512 devices in a mesh: dp: 128 (over z, y, core), tensor: 4 (over x).
Axes of the slice: x: 4, y: 8, z: 8, core: 2. Of those that a mesh axis runs over, the one named last changes fastest.
Arguments:
- context: bfloat16 [65536, 3584], P('dp', 'tensor'), may hold values from -6 to 6
- residual: bfloat16 [65536, 3584], P(('dp', 'tensor')), may hold values from -6 to 6
- out_weight: bfloat16 [3584, 3584], P('tensor', 'dp'), may hold values from -0.09375 to 0.09375
- norm_gain: float32 [3584], replicated, may hold values from 0.25 to 1.75
- members: bfloat16 [128, 512, 3584], P('dp', None, 'tensor'), may hold values from -6 to 6
- doc_lengths: int32 [512, 32], P(('dp', 'tensor')), may hold values from 1 to 12, 128 in all within a row
- doc_cluster: int32 [16384, 1], P('dp'), may hold values from 0 to 127; in each aligned block of 128 rows (0 to 127, 128 to 255, ...) at most 2 rows name the same one
- owner_map: int32 [128], replicated, may hold values from 0 to 127, each once
- member_counts: int32 [128], replicated, may hold values from 128 to 512, as said below
Outputs:
- match_scores: float32 [16384, 512], P('dp', 'tensor')
- best_match: float32 [16384], P('dp')
The draws below stay inside these ranges and needn't reach their ends.
Inputs may be any that keep to these rules, and one draw needn't show every extreme that they name: `doc_cluster`: among the documents of one index of dp (aligned blocks of 128 rows), at most 2 name the same cluster, and exactly 2 do so in some block. `member_counts`: each a multiple of 128; some cluster has exactly 512. `owner_map`: each index of dp appears once. `doc_lengths`: each row sums to 128; its largest entry is 12.
All inputs are finite; a program needn't handle non-finite values.
Results may differ from the reference program's by a relative error of at most 0.022.
Values may be sent and summed in bfloat16 or wider, within the bound.
No kernel may reach another device: no remote copies, remote signals or barrier semaphores. Data moves between devices by JAX's collectives and lax.ppermute only.
A program may use at most 64 MiB of HBM per device.

```python
import math
import jax
import jax.numpy as jnp
import numpy as np
from jax import lax

D = 3584
PACK = 128
DOC_PACK = 32
LONGEST = 12
BLOCK = 128
MAXM = 512
TOK_DEV = 512
DOC_DEV = 128
TOKENS = 65536
NPACKS = 512
DOCS = 16384
CLUSTERS = 128
CAP = 2
N_DP = 128
N_TENSOR = 4


def draw_member_counts(key, part):
    key = jax.random.fold_in(key, 11)
    key_blocks, key_index = jax.random.split(key)
    counted = jax.random.randint(key_blocks, (CLUSTERS,), 1, MAXM // BLOCK + 1) * BLOCK
    fullest = jax.random.randint(key_index, (), 0, CLUSTERS)
    return counted.at[fullest].set(MAXM).astype(jnp.int32)


def shard_levels(key, shape, cuts, least, top_value):
    def one(position, parts):
        draws = jax.random.uniform(jax.random.fold_in(jax.random.fold_in(key, 6), position), (parts,), jnp.float32, least / len(cuts), top_value / len(cuts))
        return jnp.repeat(jnp.exp(draws), shape[position] // parts).reshape((-1,) + (1,) * (len(shape) - position - 1))

    loudness = one(*cuts[0])
    for cut in cuts[1:]:
        loudness = loudness * one(*cut)
    return loudness


def split_up(count, total, reach, lean):
    weights = [(1 << 20) // math.isqrt(standing ** lean) + 1 for standing in range(2, count + 1)]
    spare, counts = total - reach - (count - 1), [1] * (count - 1)
    while spare > 0:
        candidates = [i for i in range(count - 1) if counts[i] < reach]
        pool, remaining = sum([weights[i] for i in candidates]), spare
        for i in candidates:
            more = min(reach - counts[i], max(1, remaining * weights[i] // pool), spare)
            counts[i] = counts[i] + more
            spare = spare - more
    return np.array([reach] + counts)


def uneven(stream_key, number_of, total, reach, lean):
    if number_of == 2:
        one = jax.random.randint(stream_key, (), max(1, total - reach), min(reach, total - 1) + 1)
        return jnp.stack([one, total - one])
    tallies = jnp.asarray(split_up(number_of, total, reach, lean), jnp.int32)
    pairs = (number_of - 1) // 2
    donor, receiver = tallies[1:1 + 2 * pairs:2], tallies[2:2 + 2 * pairs:2]
    slack = jnp.minimum(donor - 1, reach - receiver)
    passed = jax.random.randint(jax.random.fold_in(stream_key, 1), (pairs,), 0, 1 << 20) % (slack + 1)
    tallies = tallies.at[1:1 + 2 * pairs:2].set(donor - passed).at[2:2 + 2 * pairs:2].set(receiver + passed)
    return tallies[jax.random.permutation(jax.random.fold_in(stream_key, 2), number_of)]


def assign_block(key, own, number, rows, count, top, reach, lean):
    order = jax.random.permutation(key, count)
    heavy_load, ordinary = portions_of(count, rows * top, reach, lean, True), portions_of(count, rows * top, reach, lean, False)
    places = jnp.arange(count)

    def named(sizes, rotation):
        used = int((sizes > 0).sum())
        fixed = max(1, used // 4)
        passed = fixed + (places - fixed + rotation * (used - fixed)) % max(1, count - fixed)
        return jnp.zeros((count,), jnp.int32).at[order[jnp.where(places < fixed, places, passed)]].set(jnp.asarray(sizes, jnp.int32))

    sizes = jnp.where(number % 4 == 0, named(heavy_load, number // 4), named(ordinary, number - number // 4 - 1))
    mixed = jax.random.permutation(jax.random.fold_in(own, 3), count)
    donor, sink = mixed[0:count // 2 * 2:2], mixed[1:count // 2 * 2:2]
    room = jnp.minimum(sizes[donor] - 1, reach - sizes[sink]) // 2
    room = jnp.where((donor == order[0]) | (sink == order[0]) | (sizes[sink] == 0), 0, jnp.maximum(room, 0))
    passed = jax.random.randint(jax.random.fold_in(own, 4), (count // 2,), 0, 1 << 20) % (room + 1)
    sizes = sizes.at[donor].add(-passed).at[sink].add(passed)
    items = jnp.searchsorted(jnp.cumsum(sizes), jnp.arange(rows * top), side="right").astype(jnp.int32)
    grid = items.reshape(top, rows).T
    grid = grid[jax.random.permutation(jax.random.fold_in(own, 1), rows)]
    rotation = jax.random.randint(jax.random.fold_in(own, 2), (rows, 1), 0, top)
    return jnp.take_along_axis(grid, (jnp.arange(top)[None, :] + rotation) % top, axis=1)


def portions_of(amount, total, limit, slope, full):
    weights = [(1 << 20) // math.isqrt(rank ** slope) + 1 for rank in range(1, amount + 1)]
    largest = limit if full else min(limit, max(-(-total // amount), total * weights[0] // sum(weights)))
    least = 1 if total - largest >= amount - 1 else 0
    holding, rest = [largest] + [least] * (amount - 1), total - largest - least * (amount - 1)
    while rest > 0:
        candidates = [i for i in range(1, amount) if holding[i] < largest] or [i for i in range(1, amount) if holding[i] < limit]
        pool, remaining = sum([weights[i] for i in candidates]), rest
        for i in candidates:
            extra = min(limit - holding[i], max(1, remaining * weights[i] // pool), rest)
            holding[i] = holding[i] + extra
            rest = rest - extra
    return np.array(holding)


def noise(key, dims, deviation, bound, cuts=(), held_as=jnp.bfloat16):
    array = jax.random.normal(key, dims, jnp.float32) * deviation
    if len(cuts) > 0:
        array = shard_levels(key, dims, cuts, -0.22, 0.18) * array
    return jnp.clip(array, min=-bound, max=bound).astype(held_as)


def setup_inputs(seed: int = 0) -> dict:
    streams_of = jax.random.split(jax.random.key(seed), 10)
    context = noise(streams_of[0], (TOKENS, D), 1.0, 6.0, ((0, 128), (1, 4)))
    residual = noise(streams_of[1], (TOKENS, D), 1.0, 6.0, ((0, 512),))
    out_weight = noise(streams_of[2], (D, D), D ** -0.5, 0.09375, ((0, 4), (1, 128)))
    norm_gain = jnp.clip(1.0 + 0.15 * jax.random.normal(streams_of[3], (D,), jnp.float32), 0.25, 1.75)
    members = noise(streams_of[4], (CLUSTERS, MAXM, D), 1.0, 6.0, ((0, 128), (2, 4)))
    doc_lengths = jax.vmap(lambda own: uneven(own, DOC_PACK, PACK, LONGEST, 2))(jax.random.split(streams_of[5], NPACKS)).reshape((NPACKS, DOC_PACK)).astype(jnp.int32)
    doc_cluster_keys = jax.random.split(jax.random.fold_in(streams_of[6], 1), DOCS // DOC_DEV)
    doc_cluster_turns = jax.random.permutation(jax.random.fold_in(streams_of[6], 3), DOCS // DOC_DEV)
    doc_cluster = jax.vmap(lambda own, number: assign_block(jax.random.fold_in(streams_of[6], 2), own, number, DOC_DEV, CLUSTERS, 1, CAP, 2))(doc_cluster_keys, doc_cluster_turns).reshape((DOCS, 1))
    owner_map = jax.random.permutation(streams_of[7], CLUSTERS).astype(jnp.int32)
    member_counts = draw_member_counts(jax.random.fold_in(streams_of[9], 71), 0)
    return dict(context=context, residual=residual, out_weight=out_weight, norm_gain=norm_gain, members=members, doc_lengths=doc_lengths, doc_cluster=doc_cluster, owner_map=owner_map, member_counts=member_counts)


def rounded_sum(parts_list):
    total_sum = jnp.zeros(parts_list[0].shape, jnp.float32)
    for each_part in parts_list:
        kept = lax.optimization_barrier(each_part.astype(jnp.bfloat16))
        total_sum = total_sum + kept.astype(jnp.float32)
    return total_sum

def reference(context, residual, out_weight, norm_gain, members, doc_lengths, doc_cluster, owner_map, member_counts):
    quarter = D // N_TENSOR
    context_groups = context.reshape(N_DP, TOK_DEV, D)
    residual_groups = residual.reshape(N_DP, TOK_DEV, D)

    def project_group(pair_args):
        ctx_rows, res_rows = pair_args
        partials = []
        for index_q in range(N_TENSOR):
            lower = index_q * quarter
            partials.append(jnp.dot(ctx_rows[:, lower:lower + quarter], out_weight[lower:lower + quarter, :], preferred_element_type=jnp.float32))
        hidden = res_rows.astype(jnp.float32) + rounded_sum(partials)
        scale_rms = lax.rsqrt(lax.optimization_barrier(jnp.mean(hidden * hidden, axis=-1, keepdims=True)) + 1e-06)
        return (hidden * scale_rms * norm_gain.astype(jnp.float32)).astype(jnp.bfloat16)
    normed = lax.map(project_group, (context_groups, residual_groups)).reshape(NPACKS, PACK, D)
    ends = jnp.cumsum(doc_lengths, axis=1)
    starts = ends - doc_lengths
    positions = jnp.arange(PACK, dtype=jnp.int32)
    inside = (positions[None, None, :] >= starts[:, :, None]) & (positions[None, None, :] < ends[:, :, None])
    weights = inside.astype(jnp.float32)
    pooled = jnp.einsum('npk,nkd->npd', weights, normed.astype(jnp.float32))
    pooled = pooled / doc_lengths.astype(jnp.float32)[:, :, None]
    embedded = pooled * lax.rsqrt(lax.optimization_barrier(jnp.sum(pooled * pooled, axis=-1, keepdims=True)) + 1e-06)
    embedded = embedded.astype(jnp.bfloat16).reshape(DOCS, D)

    def member_squares(block_rows):
        parts_sq = []
        for index_q in range(N_TENSOR):
            piece_rows = block_rows[:, index_q * quarter:(index_q + 1) * quarter].astype(jnp.float32)
            parts_sq.append(lax.optimization_barrier(jnp.sum(piece_rows * piece_rows, axis=-1)))
        return rounded_sum(parts_sq)
    member_sq = lax.map(member_squares, members)
    clusters_doc = doc_cluster[:, 0]
    owners_doc = owner_map[clusters_doc]
    counts_doc = member_counts[clusters_doc]
    batches = DOCS // DOC_PACK

    def rate_batch(batch_args):
        emb_rows, owner_rows, count_rows = batch_args
        blocks = members[owner_rows]
        parts_dot = []
        for index_q in range(N_TENSOR):
            lower = index_q * quarter
            parts_dot.append(jnp.einsum('bd,bmd->bm', emb_rows[:, lower:lower + quarter].astype(jnp.float32), blocks[:, :, lower:lower + quarter].astype(jnp.float32)))
        dots = rounded_sum(parts_dot)
        scaled = dots * lax.rsqrt(member_sq[owner_rows] / D + 1e-06)
        columns = jnp.arange(MAXM, dtype=jnp.int32)
        live_cols = columns[None, :] < count_rows[:, None]
        scores = jnp.where(live_cols, scaled, 0.0)
        best = lax.optimization_barrier(jnp.max(jnp.where(live_cols, scaled, -1000000000.0), axis=-1))
        return (scores, best)
    scores, best = lax.map(rate_batch, (embedded.reshape(batches, DOC_PACK, D), owners_doc.reshape(batches, DOC_PACK), counts_doc.reshape(batches, DOC_PACK)))
    return (scores.reshape(DOCS, MAXM), best.reshape(DOCS))
```

```python
import jax
import jax.numpy as jnp
from jax import lax
from jax.experimental import pallas as pl
from jax.experimental.pallas import tpu as pltpu
from jax.sharding import Mesh, PartitionSpec as P

DP = ("z", "y", "core")
ALL = ("z", "y", "core", "tensor")
SIZES = {"z": 8, "y": 8, "core": 2, "tensor": 4}
BF = jnp.bfloat16
F32 = jnp.float32
NT = (((1,), (1,)), ((), ()))
VMEM = pl.BlockSpec(memory_space=pltpu.VMEM)
SMEM = pl.BlockSpec(memory_space=pltpu.SMEM)
TOK, QUARTER, HALF, KPIECE, KSTEP = 512, 896, 448, 512, 384
DOCS, SLOTS, MEMBERS, SHARE = 128, 256, 512, 128


def params():
    return pltpu.CompilerParams(vmem_limit_bytes=40 * 1024 * 1024)


def cost(flops, nbytes):
    return pl.CostEstimate(flops=flops, bytes_accessed=nbytes, transcendentals=0)


def shift(value, axis, step):
    size = SIZES[axis]
    return lax.ppermute(value, axis, [(i, (i + step) % size) for i in range(size)])


def spread(flip):
    pairs = []
    for z in range(8):
        for y in range(8):
            for core in range(2):
                for x in range(4):
                    source = ((z * 8 + y) * 2 + core) * 4 + x
                    target = (((2 * x + z % 2) * 8 + y) * 2 + (core ^ flip)) * 4 + z // 2
                    pairs.append((source, target))
    return pairs


def others(value):
    return shift(value, "tensor", 1), shift(value, "tensor", -1), shift(value, "tensor", 2)


def project_kernel(place, ctx, res, *refs):
    own, swapped = refs[0:9], refs[9:18]
    hidden, squares, total = refs[18:]
    z, core = place[0], place[1]
    lane_own = pl.multiple_of(core * KSTEP, 128)
    lane_other = pl.multiple_of((1 - core) * KSTEP, 128)
    total[...] = jnp.zeros_like(total)
    steps = [0, -1, 1, -2, 2, -3, 3]
    for index, step in enumerate(steps):
        at = lax.rem(z + step + 8, 8)
        quarter, half = lax.div(at, 2), lax.rem(at, 2)
        total[half] += lax.dot_general(
            ctx[quarter, :, pl.ds(lane_own, KPIECE)], own[index][...], NT, preferred_element_type=F32
        ) + lax.dot_general(
            ctx[quarter, :, pl.ds(lane_other, KPIECE)], swapped[index][...], NT, preferred_element_type=F32
        )
    at = lax.rem(z + 4, 8)
    quarter, half = lax.div(at, 2), lax.rem(at, 2)
    last_own = jnp.concatenate([own[7][...], own[8][...]], axis=0)
    last_swapped = jnp.concatenate([swapped[7][...], swapped[8][...]], axis=0)
    total[half] += lax.dot_general(
        ctx[quarter, :, pl.ds(lane_own, KPIECE)], last_own, NT, preferred_element_type=F32
    ) + lax.dot_general(
        ctx[quarter, :, pl.ds(lane_other, KPIECE)], last_swapped, NT, preferred_element_type=F32
    )
    for pack in range(4):
        rows = pl.ds(pack * 128, 128)
        value = jnp.concatenate([total[0, rows, :], total[1, rows, :]], axis=1)
        value = value + res[rows, :].astype(F32)
        hidden[rows, :] = value
        sq = value * value
        part = sq[:, 0:128]
        for tile in range(1, 7):
            part = part + sq[:, tile * 128 : tile * 128 + 128]
        squares[pl.ds(pack, 1), :] = jnp.sum(part.T, axis=0, keepdims=True)
    squares[pl.ds(4, 4), :] = jnp.zeros((4, 128), F32)


def pool_kernel(hidden, gain, pool, inverse, sq0, sq1, sq2, sq3, slots, squares):
    total = (sq0[...] + sq1[...]) + (sq2[...] + sq3[...])
    scale = lax.rsqrt(total / 3584.0 + 1e-06)
    summed = None
    for pack in range(4):
        rows = pl.ds(pack * 128, 128)
        column = jnp.broadcast_to(scale[pack : pack + 1, :], (128, 128)).T
        column = jnp.concatenate([column] * 7, axis=1)
        normed = (hidden[rows, :] * column * gain[...]).astype(BF)
        term = jnp.dot(pool[:, pack * 128 : pack * 128 + 128], normed, preferred_element_type=F32)
        summed = term if summed is None else summed + term
    pooled = summed * jnp.concatenate([inverse[...]] * 7, axis=1)
    slots[...] = pooled.astype(BF)
    sq = pooled * pooled
    part = sq[:, 0:128]
    for tile in range(1, 7):
        part = part + sq[:, tile * 128 : tile * 128 + 128]
    squares[...] = jnp.zeros_like(squares)
    for block in range(2):
        squares[pl.ds(block, 1), :] = jnp.sum(
            part[block * 128 : block * 128 + 128, :].T, axis=0, keepdims=True
        )


def dots_kernel(place, arrived, members, factor, *outs):
    x = place[2]
    for step in range(4):
        at = lax.rem(x + step, 4)
        rows = pl.ds(pl.multiple_of(at * SHARE, SHARE), SHARE)
        dots = lax.dot_general(arrived[...], members[rows, :], NT, preferred_element_type=F32)
        outs[step][...] = (dots * factor[pl.ds(at, 1), :]).astype(BF)


def home_kernel(returned, pick, scale, live, scores, best):
    rows = jnp.dot(pick[...], returned[...], preferred_element_type=F32) * scale[...]
    scores[...] = rows
    masked = jnp.where(live[...] > 0.0, rows, -1000000000.0)
    best[...] = jnp.broadcast_to(jnp.max(masked.T, axis=0, keepdims=True), (8, 128))


def body(
    context,
    residual,
    out_weight,
    norm_gain,
    members,
    doc_lengths,
    doc_cluster,
    owner_map,
    member_counts,
):
    z, y = lax.axis_index("z"), lax.axis_index("y")
    core, x = lax.axis_index("core"), lax.axis_index("tensor")
    place = jnp.stack([z, core, x]).astype(jnp.int32)

    weight = out_weight.T
    lanes = lax.broadcasted_iota(jnp.int32, (28, KPIECE), 1)
    low = weight[:, :KPIECE]
    high = jnp.where(lanes < 128, 0, weight[:, KSTEP:])
    keep = lax.ppermute(jnp.where(core == 0, low, high), ALL, spread(0))
    cross = lax.ppermute(jnp.where(core == 0, high, low), ALL, spread(1))
    block = jnp.concatenate(
        [jnp.where(core == 0, keep, cross), jnp.where(core == 0, cross, keep)], axis=0
    )

    ctx_down, ctx_up = shift(context, "tensor", 1), shift(context, "tensor", -1)

    below, above = shift(block, "y", 1), shift(block, "y", -1)
    far_below = shift(jnp.concatenate([below, block, above], axis=0), "y", 3)
    far_above = shift(jnp.concatenate([below, block], axis=0), "y", -3)
    around = jnp.concatenate([far_below, below, block, above, far_above], axis=0)
    around = jnp.concatenate([around, around], axis=0)
    begin = lax.rem(4 - y + 8, 8) * 56
    plane = lax.dynamic_slice(around, (begin, 0), (HALF, KPIECE))

    res_parts = [
        lax.dynamic_slice(residual, (0, lax.rem(x + step, 4) * QUARTER), (128, QUARTER))
        for step in range(4)
    ]
    res_recv = [
        res_parts[0],
        shift(res_parts[1], "tensor", 1),
        shift(res_parts[2], "tensor", 2),
        shift(res_parts[3], "tensor", 3),
    ]
    res = jnp.zeros((TOK, QUARTER), BF)
    for step in range(4):
        res = lax.dynamic_update_slice(res, res_recv[step], (lax.rem(x - step + 4, 4) * 128, 0))

    resident = members[0]
    resident_f = resident.astype(F32)
    partial_sq = jnp.sum(resident_f * resident_f, axis=-1).reshape(4, 128)
    lens_row = jnp.pad(doc_lengths.astype(F32), ((0, 3), (0, 96)))
    small = jnp.concatenate([partial_sq, lens_row], axis=0)
    small_down, small_up, small_far = others(small)
    member_sq = (partial_sq + small_down[:4]) + (small_up[:4] + small_far[:4])
    lens = jnp.zeros((4, 32), F32)
    for step, value in ((0, small), (3, small_down), (1, small_up), (2, small_far)):
        lens = lax.dynamic_update_slice(lens, value[4:5, :32], (lax.rem(x + step, 4), 0))

    downs, ups = [], []
    down, up = plane, plane
    for _ in range(3):
        down, up = shift(down, "z", 1), shift(up, "z", -1)
        downs.append(down)
        ups.append(up)
    half_rows = HALF // 2
    last_a = shift(downs[2][:half_rows], "z", 1)
    last_b = shift(ups[2][half_rows:], "z", -1)
    own = [plane, downs[0], ups[0], downs[1], ups[1], downs[2], ups[2], last_a, last_b]
    swapped = [shift(value, "core", 1) for value in own]

    far_a = shift(ctx_down[: TOK // 2], "tensor", 1)
    far_b = shift(ctx_up[TOK // 2 :], "tensor", -1)
    ctx = jnp.zeros((4, TOK, QUARTER), BF)
    ctx = lax.dynamic_update_slice(ctx, context[None], (x, 0, 0))
    ctx = lax.dynamic_update_slice(ctx, ctx_down[None], (lax.rem(x + 3, 4), 0, 0))
    ctx = lax.dynamic_update_slice(ctx, ctx_up[None], (lax.rem(x + 1, 4), 0, 0))
    ctx = lax.dynamic_update_slice(ctx, far_a[None], (lax.rem(x + 2, 4), 0, 0))
    ctx = lax.dynamic_update_slice(ctx, far_b[None], (lax.rem(x + 2, 4), TOK // 2, 0))

    cluster_ids = jnp.arange(owner_map.shape[0], dtype=jnp.int32)
    matches = doc_cluster[:, 0][:, None] == cluster_ids[None, :]
    doc_owner = jnp.sum(jnp.where(matches, owner_map[None, :], 0), axis=1)
    doc_members = jnp.sum(jnp.where(matches, member_counts[None, :], 0), axis=1)
    doc_order = jnp.arange(DOCS, dtype=jnp.int32)
    same_owner = (doc_owner[:, None] == doc_owner[None, :]) & (
        doc_order[:, None] > doc_order[None, :]
    )
    doc_slot = doc_owner * 2 + jnp.sum(same_owner.astype(jnp.int32), axis=1)
    slot_ids = jnp.arange(SLOTS, dtype=jnp.int32)
    select = slot_ids[:, None] == doc_slot[None, :]
    pick = (doc_slot[:, None] == slot_ids[None, :]).astype(BF)
    lens_int = lens.astype(jnp.int32)
    ends = jnp.cumsum(lens_int, axis=1)
    offsets = 128 * jnp.arange(4, dtype=jnp.int32)[:, None]
    doc_begin = (ends - lens_int + offsets).reshape(DOCS)
    doc_end = (ends + offsets).reshape(DOCS)
    tokens = jnp.arange(TOK, dtype=jnp.int32)
    inside = (tokens[None, :] >= doc_begin[:, None]) & (tokens[None, :] < doc_end[:, None])
    pool = jnp.dot(select.astype(BF), inside.astype(BF), preferred_element_type=F32).astype(BF)
    slot_len = jnp.sum(jnp.where(select, lens.reshape(DOCS)[None, :], 0.0), axis=1)
    inverse = jnp.broadcast_to((1.0 / jnp.maximum(slot_len, 1.0))[:, None], (SLOTS, 128))
    columns = x * SHARE + jnp.arange(SHARE, dtype=jnp.int32)
    live = (columns[None, :] < doc_members[:, None]).astype(F32)

    own_dp = (z * 8 + y) * 2 + core
    own_count = jnp.sum(jnp.where(owner_map == own_dp, member_counts, 0))
    member_ids = jnp.arange(MEMBERS, dtype=jnp.int32).reshape(4, 128)
    factor = jnp.where(member_ids < own_count, lax.rsqrt(member_sq / 3584.0 + 1e-06), 0.0)

    hidden, squares = pl.pallas_call(
        project_kernel,
        out_shape=(
            jax.ShapeDtypeStruct((TOK, QUARTER), F32),
            jax.ShapeDtypeStruct((8, 128), F32),
        ),
        in_specs=[SMEM] + [VMEM] * 20,
        out_specs=(VMEM, VMEM),
        scratch_shapes=[pltpu.VMEM((2, TOK, HALF), F32)],
        compiler_params=params(),
        cost_estimate=cost(2 * TOK * QUARTER * 4096, 16_000_000),
        name="project",
    )(place, ctx, res, *own, *swapped)

    slots, doc_sq = pl.pallas_call(
        pool_kernel,
        out_shape=(
            jax.ShapeDtypeStruct((SLOTS, QUARTER), BF),
            jax.ShapeDtypeStruct((8, 128), F32),
        ),
        in_specs=[VMEM] * 8,
        out_specs=(VMEM, VMEM),
        compiler_params=params(),
        cost_estimate=cost(2 * SLOTS * TOK * QUARTER, 3_000_000),
        name="pool",
    )(hidden, gain_of(norm_gain, x), pool, inverse, squares, *others(squares))

    arrived = lax.all_to_all(
        slots.reshape(DOCS, 2, QUARTER), DP, split_axis=0, concat_axis=0, tiled=True
    ).reshape(SLOTS, QUARTER)

    doc_sq_all = [doc_sq, *others(doc_sq)]
    slot_sq = sum(doc_sq_all[1:], doc_sq_all[0])[:2].reshape(SLOTS)
    doc_total = jnp.sum(jnp.where(select, slot_sq[:, None], 0.0), axis=0)
    scale = jnp.broadcast_to(lax.rsqrt(doc_total + 1e-06)[:, None], (DOCS, SHARE))

    partials = pl.pallas_call(
        dots_kernel,
        out_shape=tuple(jax.ShapeDtypeStruct((SLOTS, SHARE), BF) for _ in range(4)),
        in_specs=[SMEM] + [VMEM] * 3,
        out_specs=(VMEM,) * 4,
        compiler_params=params(),
        cost_estimate=cost(2 * SLOTS * MEMBERS * QUARTER, 2_000_000),
        name="dots",
    )(place, arrived, resident, factor)
    received = [partials[0]] + [shift(partials[step], "tensor", step) for step in range(1, 4)]
    scored = sum((value.astype(F32) for value in received[1:]), received[0].astype(F32)).astype(BF)

    returned = lax.all_to_all(
        scored.reshape(DOCS, 2, SHARE), DP, split_axis=0, concat_axis=0, tiled=True
    ).reshape(SLOTS, SHARE)
    scores, best = pl.pallas_call(
        home_kernel,
        out_shape=(
            jax.ShapeDtypeStruct((DOCS, SHARE), F32),
            jax.ShapeDtypeStruct((8, 128), F32),
        ),
        in_specs=[VMEM] * 4,
        out_specs=(VMEM, VMEM),
        compiler_params=params(),
        cost_estimate=cost(2 * SLOTS * DOCS * SHARE, 400_000),
        name="home",
    )(returned, pick, scale, live)
    best_down, best_up, best_far = others(best)
    best = jnp.maximum(jnp.maximum(best, best_down), jnp.maximum(best_up, best_far))
    return scores, best[0]


def gain_of(norm_gain, x):
    return lax.dynamic_slice(norm_gain, (x * QUARTER,), (QUARTER,)).reshape(1, QUARTER)


def solution(mesh):
    split = Mesh(mesh.devices.reshape(8, 8, 2, 4), ALL)
    in_specs = (
        P(DP, "tensor"),
        P(ALL, None),
        P("tensor", DP),
        P(),
        P(DP, None, "tensor"),
        P(ALL, None),
        P(DP, None),
        P(),
        P(),
    )
    out_specs = (P(DP, "tensor"), P(DP))
    return jax.shard_map(body, mesh=split, in_specs=in_specs, out_specs=out_specs, check_vma=False)
```

```python
import jax
import jax.numpy as jnp
from jax import lax
from jax.experimental import pallas as pl
from jax.experimental.pallas import tpu as pltpu
from jax.sharding import Mesh, PartitionSpec as P

DP = ("z", "y", "core")
ALL = ("z", "y", "core", "tensor")
SIZES = {"z": 8, "y": 8, "core": 2, "tensor": 4}
BF = jnp.bfloat16
F32 = jnp.float32
NT = (((1,), (1,)), ((), ()))
VMEM = pl.BlockSpec(memory_space=pltpu.VMEM)
TOK, QUARTER, HALF = 512, 896, 448
DOCS, SLOTS, MEMBERS, SHARE = 128, 256, 512, 128


def params():
    return pltpu.CompilerParams(vmem_limit_bytes=40 * 1024 * 1024)


def cost(flops, nbytes):
    return pl.CostEstimate(flops=flops, bytes_accessed=nbytes, transcendentals=0)


def shift(value, axis, step):
    size = SIZES[axis]
    return lax.ppermute(value, axis, [(i, (i + step) % size) for i in range(size)])


def spread(flip):
    pairs = []
    for z in range(8):
        for y in range(8):
            for core in range(2):
                for x in range(4):
                    source = ((z * 8 + y) * 2 + core) * 4 + x
                    target = (((2 * x + z % 2) * 8 + y) * 2 + (core ^ flip)) * 4 + z // 2
                    pairs.append((source, target))
    return pairs


def project_kernel(ctx, weight, res, hidden, squares, total):
    step = pl.program_id(0)
    half = lax.rem(step, 2)
    product = lax.dot_general(ctx[0], weight[...], NT, preferred_element_type=F32)

    @pl.when(step < 2)
    def _():
        total[half] = product

    @pl.when(step >= 2)
    def _():
        total[half] += product

    @pl.when(step == 7)
    def _():
        for pack in range(4):
            rows = pl.ds(pack * 128, 128)
            value = jnp.concatenate([total[0, rows, :], total[1, rows, :]], axis=1)
            value = value + res[rows, :].astype(F32)
            hidden[rows, :] = value
            sq = value * value
            part = sq[:, 0:128]
            for tile in range(1, 7):
                part = part + sq[:, tile * 128 : tile * 128 + 128]
            squares[pl.ds(pack, 1), :] = jnp.sum(part.T, axis=0, keepdims=True)
        squares[pl.ds(4, 4), :] = jnp.zeros((4, 128), F32)


def pool_kernel(hidden, gain, pool, inverse, total, slots, squares):
    scale = lax.rsqrt(total[...] / 3584.0 + 1e-06)
    summed = None
    for pack in range(4):
        rows = pl.ds(pack * 128, 128)
        column = jnp.broadcast_to(scale[pack : pack + 1, :], (128, 128)).T
        column = jnp.concatenate([column] * 7, axis=1)
        normed = (hidden[rows, :] * column * gain[...]).astype(BF)
        term = jnp.dot(pool[:, pack * 128 : pack * 128 + 128], normed, preferred_element_type=F32)
        summed = term if summed is None else summed + term
    pooled = summed * jnp.concatenate([inverse[...]] * 7, axis=1)
    slots[...] = pooled.astype(BF)
    sq = pooled * pooled
    part = sq[:, 0:128]
    for tile in range(1, 7):
        part = part + sq[:, tile * 128 : tile * 128 + 128]
    squares[...] = jnp.zeros_like(squares)
    for block in range(2):
        squares[pl.ds(block, 1), :] = jnp.sum(
            part[block * 128 : block * 128 + 128, :].T, axis=0, keepdims=True
        )


def dots_kernel(arrived, members, factor, out):
    for part in range(4):
        rows = pl.ds(part * SHARE, SHARE)
        dots = lax.dot_general(arrived[...], members[rows, :], NT, preferred_element_type=F32)
        out[:, part * SHARE : part * SHARE + SHARE] = (dots * factor[pl.ds(part, 1), :]).astype(BF)


def home_kernel(returned, pick, scale, live, scores, best):
    rows = jnp.dot(pick[...], returned[...], preferred_element_type=F32) * scale[...]
    scores[...] = rows
    masked = jnp.where(live[...] > 0.0, rows, -1000000000.0)
    best[...] = jnp.broadcast_to(jnp.max(masked.T, axis=0, keepdims=True), (8, 128))


def body(
    context,
    residual,
    out_weight,
    norm_gain,
    members,
    doc_lengths,
    doc_cluster,
    owner_map,
    member_counts,
):
    z, y = lax.axis_index("z"), lax.axis_index("y")
    core, x = lax.axis_index("core"), lax.axis_index("tensor")

    weight = out_weight.T
    keep = lax.ppermute(weight, ALL, spread(0))
    cross = lax.ppermute(weight, ALL, spread(1))
    block = jnp.concatenate(
        [jnp.where(core == 0, keep, cross), jnp.where(core == 0, cross, keep)], axis=0
    )
    context, residual, doc_lengths, block = lax.optimization_barrier(
        (context, residual, doc_lengths, block)
    )
    plane = lax.all_gather(block, ("z", "y"), axis=0, tiled=True)

    ctx_down, ctx_up = shift(context, "tensor", 1), shift(context, "tensor", -1)

    res_parts = [
        lax.dynamic_slice(residual, (0, lax.rem(x + step, 4) * QUARTER), (128, QUARTER))
        for step in range(4)
    ]
    res_recv = [
        res_parts[0],
        shift(res_parts[1], "tensor", 1),
        shift(res_parts[2], "tensor", 2),
        shift(res_parts[3], "tensor", 3),
    ]
    res = jnp.zeros((TOK, QUARTER), BF)
    for step in range(4):
        res = lax.dynamic_update_slice(res, res_recv[step], (lax.rem(x - step + 4, 4) * 128, 0))

    resident = members[0]
    resident_f = resident.astype(F32)
    partial_sq = jnp.sum(resident_f * resident_f, axis=-1).reshape(4, 128)
    lens_rows = jnp.zeros((4, 128), F32)
    lens_rows = lax.dynamic_update_slice(lens_rows, doc_lengths.astype(F32), (x, 0))
    small = lax.psum(jnp.concatenate([partial_sq, lens_rows], axis=0), "tensor")
    small, res = lax.optimization_barrier((small, res))
    member_sq, lens = small[:4], small[4:, :32]

    far_a = shift(ctx_down[: TOK // 2], "tensor", 1)
    far_b = shift(ctx_up[TOK // 2 :], "tensor", -1)
    ctx = jnp.zeros((4, TOK, QUARTER), BF)
    ctx = lax.dynamic_update_slice(ctx, context[None], (x, 0, 0))
    ctx = lax.dynamic_update_slice(ctx, ctx_down[None], (lax.rem(x + 3, 4), 0, 0))
    ctx = lax.dynamic_update_slice(ctx, ctx_up[None], (lax.rem(x + 1, 4), 0, 0))
    ctx = lax.dynamic_update_slice(ctx, far_a[None], (lax.rem(x + 2, 4), 0, 0))
    ctx = lax.dynamic_update_slice(ctx, far_b[None], (lax.rem(x + 2, 4), TOK // 2, 0))

    cluster_ids = jnp.arange(owner_map.shape[0], dtype=jnp.int32)
    matches = doc_cluster[:, 0][:, None] == cluster_ids[None, :]
    doc_owner = jnp.sum(jnp.where(matches, owner_map[None, :], 0), axis=1)
    doc_members = jnp.sum(jnp.where(matches, member_counts[None, :], 0), axis=1)
    doc_order = jnp.arange(DOCS, dtype=jnp.int32)
    same_owner = (doc_owner[:, None] == doc_owner[None, :]) & (
        doc_order[:, None] > doc_order[None, :]
    )
    doc_slot = doc_owner * 2 + jnp.sum(same_owner.astype(jnp.int32), axis=1)
    slot_ids = jnp.arange(SLOTS, dtype=jnp.int32)
    select = slot_ids[:, None] == doc_slot[None, :]
    wide_ids = jnp.arange(4 * SLOTS, dtype=jnp.int32)
    wide_ids = lax.div(wide_ids, 8) * 2 + lax.rem(wide_ids, 2)
    pick = (doc_slot[:, None] == wide_ids[None, :]).astype(BF)
    lens_int = lens.astype(jnp.int32)
    ends = jnp.cumsum(lens_int, axis=1)
    offsets = 128 * jnp.arange(4, dtype=jnp.int32)[:, None]
    doc_begin = (ends - lens_int + offsets).reshape(DOCS)
    doc_end = (ends + offsets).reshape(DOCS)
    tokens = jnp.arange(TOK, dtype=jnp.int32)
    inside = (tokens[None, :] >= doc_begin[:, None]) & (tokens[None, :] < doc_end[:, None])
    pool = jnp.dot(select.astype(BF), inside.astype(BF), preferred_element_type=F32).astype(BF)
    slot_len = jnp.sum(jnp.where(select, lens.reshape(DOCS)[None, :], 0.0), axis=1)
    inverse = jnp.broadcast_to((1.0 / jnp.maximum(slot_len, 1.0))[:, None], (SLOTS, 128))
    columns = x * SHARE + jnp.arange(SHARE, dtype=jnp.int32)
    live = (columns[None, :] < doc_members[:, None]).astype(F32)

    own_dp = (z * 8 + y) * 2 + core
    own_count = jnp.sum(jnp.where(owner_map == own_dp, member_counts, 0))
    member_ids = jnp.arange(MEMBERS, dtype=jnp.int32).reshape(4, 128)
    factor = jnp.where(member_ids < own_count, lax.rsqrt(member_sq / 3584.0 + 1e-06), 0.0)

    hidden, squares = pl.pallas_call(
        project_kernel,
        out_shape=(
            jax.ShapeDtypeStruct((TOK, QUARTER), F32),
            jax.ShapeDtypeStruct((8, 128), F32),
        ),
        grid=(8,),
        in_specs=[
            pl.BlockSpec((1, TOK, QUARTER), lambda i: (lax.div(i, 2), 0, 0)),
            pl.BlockSpec((HALF, QUARTER), lambda i: (i, 0)),
            pl.BlockSpec((TOK, QUARTER), lambda i: (0, 0)),
        ],
        out_specs=(
            pl.BlockSpec((TOK, QUARTER), lambda i: (0, 0)),
            pl.BlockSpec((8, 128), lambda i: (0, 0)),
        ),
        scratch_shapes=[pltpu.VMEM((2, TOK, HALF), F32)],
        compiler_params=params(),
        cost_estimate=cost(2 * TOK * QUARTER * 3584, 13_000_000),
        name="project",
    )(ctx, plane, res)

    slots, doc_sq = pl.pallas_call(
        pool_kernel,
        out_shape=(
            jax.ShapeDtypeStruct((SLOTS, QUARTER), BF),
            jax.ShapeDtypeStruct((8, 128), F32),
        ),
        in_specs=[VMEM] * 5,
        out_specs=(VMEM, VMEM),
        compiler_params=params(),
        cost_estimate=cost(2 * SLOTS * TOK * QUARTER, 3_000_000),
        name="pool",
    )(hidden, gain_of(norm_gain, x), pool, inverse, lax.psum(squares, "tensor"))

    arrived = lax.all_to_all(
        slots.reshape(DOCS, 2, QUARTER), DP, split_axis=0, concat_axis=0, tiled=True
    ).reshape(SLOTS, QUARTER)

    slot_sq = lax.psum(doc_sq, "tensor")[:2].reshape(SLOTS)
    doc_total = jnp.sum(jnp.where(select, slot_sq[:, None], 0.0), axis=0)
    scale = jnp.broadcast_to(lax.rsqrt(doc_total + 1e-06)[:, None], (DOCS, SHARE))

    partial = pl.pallas_call(
        dots_kernel,
        out_shape=jax.ShapeDtypeStruct((SLOTS, MEMBERS), BF),
        in_specs=[VMEM] * 3,
        out_specs=VMEM,
        compiler_params=params(),
        cost_estimate=cost(2 * SLOTS * MEMBERS * QUARTER, 2_000_000),
        name="dots",
    )(arrived, resident, factor)

    partial = partial.reshape(DOCS, 2, 4, SHARE).transpose(0, 2, 1, 3).reshape(4 * DOCS, 2, SHARE)
    returned = lax.all_to_all(partial, ALL, split_axis=0, concat_axis=0, tiled=True)
    returned = returned.reshape(4 * SLOTS, SHARE)
    scores, best = pl.pallas_call(
        home_kernel,
        out_shape=(
            jax.ShapeDtypeStruct((DOCS, SHARE), F32),
            jax.ShapeDtypeStruct((8, 128), F32),
        ),
        in_specs=[VMEM] * 4,
        out_specs=(VMEM, VMEM),
        compiler_params=params(),
        cost_estimate=cost(2 * SLOTS * DOCS * SHARE, 400_000),
        name="home",
    )(returned, pick, scale, live)
    return scores, lax.pmax(best[0], "tensor")


def gain_of(norm_gain, x):
    return lax.dynamic_slice(norm_gain, (x * QUARTER,), (QUARTER,)).reshape(1, QUARTER)


def solution(mesh):
    split = Mesh(mesh.devices.reshape(8, 8, 2, 4), ALL)
    in_specs = (
        P(DP, "tensor"),
        P(ALL, None),
        P("tensor", DP),
        P(),
        P(DP, None, "tensor"),
        P(ALL, None),
        P(DP, None),
        P(),
        P(),
    )
    out_specs = (P(DP, "tensor"), P(DP))
    return jax.shard_map(body, mesh=split, in_specs=in_specs, out_specs=out_specs, check_vma=False)
```

```python
import jax
import jax.numpy as jnp
from jax import lax
from jax.experimental import pallas as pl
from jax.experimental.pallas import tpu as pltpu
from jax.sharding import Mesh, PartitionSpec as P

DP = ("z", "y", "core")
ALL = ("z", "y", "core", "tensor")
BF = jnp.bfloat16
F32 = jnp.float32
NT = (((1,), (1,)), ((), ()))
SMEM = pl.BlockSpec(memory_space=pltpu.SMEM)
VMEM = pl.BlockSpec(memory_space=pltpu.VMEM)
TOK, QUARTER, HALF, WINDOW, OFFSET = 512, 896, 448, 512, 384
DOCS, SLOTS, MEMBERS, SHARE = 128, 256, 512, 128


def params():
    return pltpu.CompilerParams(vmem_limit_bytes=20 * 1024 * 1024)


def cost(flops, nbytes):
    return pl.CostEstimate(flops=flops, bytes_accessed=nbytes, transcendentals=0)


def device(z, y, core, x):
    return ((z * 8 + y) * 2 + core) * 4 + x


def placed(core, ring, line):
    return (ring, line) if core == 0 else (line, ring)


def grid():
    return [(z, y, c, x) for z in range(8) for y in range(8) for c in range(2) for x in range(4)]


def spread(flip):
    pairs = []
    for z, y, core, x in grid():
        to = core ^ flip
        to_z, to_y = placed(to, 2 * x + z % 2, y)
        pairs.append((device(z, y, core, x), device(to_z, to_y, to, z // 2)))
    return pairs


def groups(along):
    found = []
    for core in range(2):
        for x in range(4):
            for other in range(8):
                over_z = (along == "ring") == (core == 0)
                found.append(
                    [device(i, other, core, x) if over_z else device(other, i, core, x) for i in range(8)]
                )
    return found


def pair(value, turn):
    pairs = []
    for z, y, core, x in grid():
        pairs.append((device(z, y, core, x), device(z, y, core, x ^ (1 if core == turn else 3))))
    return lax.ppermute(value, ALL, pairs)


def core_swap(value):
    return lax.ppermute(value, ALL, [(at, at ^ 4) for at in range(512)])


def window(core):
    return pl.ds(pl.multiple_of(core * OFFSET, 128), WINDOW)


def pack_kernel(place, context, theirs, residual, small, near, side):
    core = place[2]
    for out in (near, side):
        out[0:TOK, :] = context[:, window(core)]
        out[TOK : 2 * TOK, :] = theirs[...]
    for out, row, target in ((near, 1024, 3), (near, 1280, 5), (side, 1024, 4)):
        start = place[target] * QUARTER
        out[row : row + 128, :] = residual[:, pl.ds(pl.multiple_of(start, 128), WINDOW)]
        out[row + 128 : row + 256, :] = residual[
            :, pl.ds(pl.multiple_of(start + OFFSET, 128), WINDOW)
        ]
    near[1536:1552, :] = small[...]
    side[1280:1296, :] = small[...]


def gather_kernel(place, context, theirs, residual, near, side, far, ctx, res):
    x = place[1]
    ctx[x, 0:TOK, :] = context[:, window(place[2])]
    ctx[x, TOK : 2 * TOK, :] = theirs[...]

    def put(at, value):
        res[pl.ds(pl.multiple_of(at * 128, 128), 128), :] = value

    put(x, residual[:, pl.ds(pl.multiple_of(x * QUARTER, 128), QUARTER)])
    for index, piece, row in ((3, near, 1024), (4, side, 1024), (5, far, 1280)):
        ctx[place[index]] = piece[0 : 2 * TOK, :]
        left, right = piece[row : row + 128, :], piece[row + 128 : row + 256, 128:512]
        put(place[index], jnp.concatenate([left, right], axis=1))


def sum_block(ctx, weight, total):
    step = pl.program_id(0)
    half = lax.rem(step, 2)
    product = lax.dot_general(ctx[0], weight[...], NT, preferred_element_type=F32)

    @pl.when(step < 2)
    def _():
        total[half] = product

    @pl.when(step >= 2)
    def _():
        total[half] += product


def whole(total, pack):
    rows = pl.ds(pack * 128, 128)
    return jnp.concatenate([total[0, rows, :], total[1, rows, :]], axis=1)


def other_kernel(ctx, weight, out, total):
    sum_block(ctx, weight, total)

    @pl.when(pl.program_id(0) == 7)
    def _():
        for pack in range(4):
            out[pl.ds(pack * 128, 128), :] = whole(total, pack).astype(BF)


def own_kernel(ctx, weight, res, out, total):
    sum_block(ctx, weight, total)

    @pl.when(pl.program_id(0) == 7)
    def _():
        for pack in range(4):
            rows = pl.ds(pack * 128, 128)
            out[rows, :] = whole(total, pack) + res[rows, :].astype(F32)


def rms_kernel(own, swapped, squares):
    squares[...] = jnp.zeros_like(squares)
    for pack in range(4):
        rows = pl.ds(pack * 128, 128)
        value = own[rows, :] + swapped[rows, :].astype(F32)
        sq = value * value
        part = sq[:, 0:128]
        for tile in range(1, 7):
            part = part + sq[:, tile * 128 : tile * 128 + 128]
        squares[pl.ds(pack, 1), :] = jnp.sum(part.T, axis=0, keepdims=True)


def pool_kernel(own, swapped, gain, pool, inverse, total, slots, squares):
    scale = lax.rsqrt(total[...] / 3584.0 + 1e-06)
    summed = None
    for pack in range(4):
        rows = pl.ds(pack * 128, 128)
        column = jnp.broadcast_to(scale[pack : pack + 1, :], (128, 128)).T
        column = jnp.concatenate([column] * 7, axis=1)
        hidden = own[rows, :] + swapped[rows, :].astype(F32)
        normed = (hidden * column * gain[...]).astype(BF)
        term = jnp.dot(pool[:, pack * 128 : pack * 128 + 128], normed, preferred_element_type=F32)
        summed = term if summed is None else summed + term
    pooled = summed * jnp.concatenate([inverse[...]] * 7, axis=1)
    slots[...] = pooled.astype(BF)
    sq = pooled * pooled
    part = sq[:, 0:128]
    for tile in range(1, 7):
        part = part + sq[:, tile * 128 : tile * 128 + 128]
    squares[...] = jnp.zeros_like(squares)
    for block in range(2):
        squares[pl.ds(block, 1), :] = jnp.sum(
            part[block * 128 : block * 128 + 128, :].T, axis=0, keepdims=True
        )


def dots_kernel(arrived, members, factor, out):
    for part in range(4):
        rows = pl.ds(part * SHARE, SHARE)
        dots = lax.dot_general(arrived[...], members[rows, :], NT, preferred_element_type=F32)
        out[:, part * SHARE : part * SHARE + SHARE] = (dots * factor[pl.ds(part, 1), :]).astype(BF)


def home_kernel(returned, pick, scale, live, scores, best):
    rows = jnp.dot(pick[...], returned[...], preferred_element_type=F32) * scale[...]
    scores[...] = rows
    masked = jnp.where(live[...] > 0.0, rows, -1000000000.0)
    best[...] = jnp.broadcast_to(jnp.max(masked.T, axis=0, keepdims=True), (8, 128))


def body(
    context,
    residual,
    out_weight,
    norm_gain,
    members,
    doc_lengths,
    doc_cluster,
    owner_map,
    member_counts,
):
    z, y = lax.axis_index("z"), lax.axis_index("y")
    core, x = lax.axis_index("core"), lax.axis_index("tensor")

    first = core == 0
    ring, line = jnp.where(first, z, y), jnp.where(first, y, z)
    near_x = jnp.where(first, x ^ 1, x ^ 3)
    side_x = jnp.where(first, x ^ 3, x ^ 1)
    far_x = x ^ 2
    place = jnp.stack([ring, x, core, near_x, side_x, far_x]).astype(jnp.int32)

    weight = out_weight.T
    lanes = lax.broadcasted_iota(jnp.int32, (28, WINDOW), 1)
    low = weight[:, :WINDOW]
    high = jnp.where(lanes < WINDOW - OFFSET, 0, weight[:, OFFSET:])
    keep = lax.ppermute(jnp.where(first, low, high), ALL, spread(0))
    cross = lax.ppermute(jnp.where(first, high, low), ALL, spread(1))
    block = jnp.concatenate(
        [jnp.where(first, keep, cross), jnp.where(first, cross, keep)], axis=0
    )

    late_context, _ = lax.optimization_barrier((context, keep))
    theirs = core_swap(jnp.where(first, late_context[:, OFFSET:], late_context[:, :WINDOW]))
    resident = members[0]
    resident_f = resident.astype(F32)
    partial_sq = jnp.sum(resident_f * resident_f, axis=-1).astype(BF)
    small = jnp.concatenate(
        [partial_sq.reshape(4, 128), jnp.pad(doc_lengths.astype(BF), ((0, 0), (0, 96)))], axis=0
    )
    small = jnp.pad(small, ((0, 11), (0, WINDOW - 128)))
    late_theirs, _ = lax.optimization_barrier((theirs, block))
    to_near, to_side = pl.pallas_call(
        pack_kernel,
        out_shape=(
            jax.ShapeDtypeStruct((1552, WINDOW), BF),
            jax.ShapeDtypeStruct((1296, WINDOW), BF),
        ),
        in_specs=[SMEM] + [VMEM] * 4,
        out_specs=(VMEM, VMEM),
        compiler_params=params(),
        cost_estimate=cost(0, 6_000_000),
        name="pack",
    )(place, context, late_theirs, residual, small)
    block, to_near = lax.optimization_barrier((block, to_near))
    near, side = pair(to_near, 0), pair(to_side, 1)
    plane = lax.all_to_all(
        jnp.broadcast_to(block[None], (8, 56, WINDOW)), ALL, 0, 0,
        axis_index_groups=groups("line"), tiled=True,
    ).reshape(HALF, WINDOW)
    plane = lax.all_gather(plane, ALL, axis=0, axis_index_groups=groups("ring"), tiled=True)
    far = pair(near, 1)

    tails = [(x, small), (near_x, near[-16:]), (side_x, side[-16:]), (far_x, far[-16:])]
    member_sq = sum((tail[:4, :128].astype(F32) for _, tail in tails[1:]), small[:4, :128].astype(F32))
    lens = jnp.zeros((4, 32), F32)
    for at, tail in tails:
        lens = lax.dynamic_update_slice(lens, tail[4:5, :32].astype(F32), (at, 0))

    cluster_ids = jnp.arange(owner_map.shape[0], dtype=jnp.int32)
    matches = doc_cluster[:, 0][:, None] == cluster_ids[None, :]
    doc_owner = jnp.sum(jnp.where(matches, owner_map[None, :], 0), axis=1)
    doc_members = jnp.sum(jnp.where(matches, member_counts[None, :], 0), axis=1)
    doc_order = jnp.arange(DOCS, dtype=jnp.int32)
    same_owner = (doc_owner[:, None] == doc_owner[None, :]) & (
        doc_order[:, None] > doc_order[None, :]
    )
    doc_slot = doc_owner * 2 + jnp.sum(same_owner.astype(jnp.int32), axis=1)
    slot_ids = jnp.arange(SLOTS, dtype=jnp.int32)
    select = slot_ids[:, None] == doc_slot[None, :]
    wide_ids = jnp.arange(4 * SLOTS, dtype=jnp.int32)
    wide_ids = lax.div(wide_ids, 8) * 2 + lax.rem(wide_ids, 2)
    pick = (doc_slot[:, None] == wide_ids[None, :]).astype(BF)
    lens_int = lens.astype(jnp.int32)
    ends = jnp.cumsum(lens_int, axis=1)
    offsets = 128 * jnp.arange(4, dtype=jnp.int32)[:, None]
    doc_begin = (ends - lens_int + offsets).reshape(DOCS)
    doc_end = (ends + offsets).reshape(DOCS)
    tokens = jnp.arange(TOK, dtype=jnp.int32)
    inside = (tokens[None, :] >= doc_begin[:, None]) & (tokens[None, :] < doc_end[:, None])
    pool = jnp.dot(select.astype(BF), inside.astype(BF), preferred_element_type=F32).astype(BF)
    slot_len = jnp.sum(jnp.where(select, lens.reshape(DOCS)[None, :], 0.0), axis=1)
    inverse = jnp.broadcast_to((1.0 / jnp.maximum(slot_len, 1.0))[:, None], (SLOTS, 128))
    columns = x * SHARE + jnp.arange(SHARE, dtype=jnp.int32)
    live = (columns[None, :] < doc_members[:, None]).astype(F32)

    own_dp = (z * 8 + y) * 2 + core
    own_count = jnp.sum(jnp.where(owner_map == own_dp, member_counts, 0))
    member_ids = jnp.arange(MEMBERS, dtype=jnp.int32).reshape(4, 128)
    factor = jnp.where(member_ids < own_count, lax.rsqrt(member_sq / 3584.0 + 1e-06), 0.0)

    ctx, res = pl.pallas_call(
        gather_kernel,
        out_shape=(
            jax.ShapeDtypeStruct((4, 2 * TOK, WINDOW), BF),
            jax.ShapeDtypeStruct((TOK, QUARTER), BF),
        ),
        in_specs=[SMEM] + [VMEM] * 6,
        out_specs=(VMEM, VMEM),
        compiler_params=params(),
        cost_estimate=cost(0, 10_000_000),
        name="gather",
    )(place, context, theirs, residual, near, side, far)
    weight_spec = pl.BlockSpec((HALF, WINDOW), lambda i: (i, 0))
    out_spec = pl.BlockSpec((TOK, QUARTER), lambda i: (0, 0))
    half_cost = cost(8 * 2 * TOK * WINDOW * HALF, 8_000_000)
    other = pl.pallas_call(
        other_kernel,
        out_shape=jax.ShapeDtypeStruct((TOK, QUARTER), BF),
        grid=(8,),
        in_specs=[pl.BlockSpec((1, TOK, WINDOW), lambda i: (lax.div(i, 2), 1, 0)), weight_spec],
        out_specs=out_spec,
        scratch_shapes=[pltpu.VMEM((2, TOK, HALF), F32)],
        compiler_params=params(),
        cost_estimate=half_cost,
        name="other",
    )(ctx, plane)
    swapped = core_swap(other)
    own = pl.pallas_call(
        own_kernel,
        out_shape=jax.ShapeDtypeStruct((TOK, QUARTER), F32),
        grid=(8,),
        in_specs=[
            pl.BlockSpec((1, TOK, WINDOW), lambda i: (lax.div(i, 2), 0, 0)),
            weight_spec,
            out_spec,
        ],
        out_specs=out_spec,
        scratch_shapes=[pltpu.VMEM((2, TOK, HALF), F32)],
        compiler_params=params(),
        cost_estimate=half_cost,
        name="own",
    )(ctx, plane, res)
    squares = pl.pallas_call(
        rms_kernel,
        out_shape=jax.ShapeDtypeStruct((8, 128), F32),
        in_specs=[VMEM] * 2,
        out_specs=VMEM,
        compiler_params=params(),
        cost_estimate=cost(2 * TOK * QUARTER, 3_000_000),
        name="rms",
    )(own, swapped)

    slots, doc_sq = pl.pallas_call(
        pool_kernel,
        out_shape=(
            jax.ShapeDtypeStruct((SLOTS, QUARTER), BF),
            jax.ShapeDtypeStruct((8, 128), F32),
        ),
        in_specs=[VMEM] * 6,
        out_specs=(VMEM, VMEM),
        compiler_params=params(),
        cost_estimate=cost(2 * SLOTS * TOK * QUARTER, 3_000_000),
        name="pool",
    )(own, swapped, gain_of(norm_gain, x), pool, inverse, lax.psum(squares, "tensor"))

    arrived = lax.all_to_all(
        slots.reshape(DOCS, 2, QUARTER), DP, split_axis=0, concat_axis=0, tiled=True
    ).reshape(SLOTS, QUARTER)

    slot_sq = lax.psum(doc_sq, "tensor")[:2].reshape(SLOTS)
    doc_total = jnp.sum(jnp.where(select, slot_sq[:, None], 0.0), axis=0)
    scale = jnp.broadcast_to(lax.rsqrt(doc_total + 1e-06)[:, None], (DOCS, SHARE))

    partial = pl.pallas_call(
        dots_kernel,
        out_shape=jax.ShapeDtypeStruct((SLOTS, MEMBERS), BF),
        in_specs=[VMEM] * 3,
        out_specs=VMEM,
        compiler_params=params(),
        cost_estimate=cost(2 * SLOTS * MEMBERS * QUARTER, 2_000_000),
        name="dots",
    )(arrived, resident, factor)

    partial = partial.reshape(DOCS, 2, 4, SHARE).transpose(0, 2, 1, 3).reshape(4 * DOCS, 2, SHARE)
    returned = lax.all_to_all(partial, ALL, split_axis=0, concat_axis=0, tiled=True)
    returned = returned.reshape(4 * SLOTS, SHARE)
    scores, best = pl.pallas_call(
        home_kernel,
        out_shape=(
            jax.ShapeDtypeStruct((DOCS, SHARE), F32),
            jax.ShapeDtypeStruct((8, 128), F32),
        ),
        in_specs=[VMEM] * 4,
        out_specs=(VMEM, VMEM),
        compiler_params=params(),
        cost_estimate=cost(2 * SLOTS * DOCS * SHARE, 400_000),
        name="home",
    )(returned, pick, scale, live)
    return scores, lax.pmax(best[0], "tensor")


def gain_of(norm_gain, x):
    return lax.dynamic_slice(norm_gain, (x * QUARTER,), (QUARTER,)).reshape(1, QUARTER)


def solution(mesh):
    split = Mesh(mesh.devices.reshape(8, 8, 2, 4), ALL)
    in_specs = (
        P(DP, "tensor"),
        P(ALL, None),
        P("tensor", DP),
        P(),
        P(DP, None, "tensor"),
        P(ALL, None),
        P(DP, None),
        P(),
        P(),
    )
    out_specs = (P(DP, "tensor"), P(DP))
    return jax.shard_map(body, mesh=split, in_specs=in_specs, out_specs=out_specs, check_vma=False)
```

```python
import jax
import jax.numpy as jnp
from jax import lax
from jax.experimental import pallas as pl
from jax.experimental.pallas import tpu as pltpu
from jax.sharding import Mesh, PartitionSpec as P

DP = ("z", "y", "core")
ALL = ("z", "y", "core", "tensor")
BF = jnp.bfloat16
F32 = jnp.float32
NT = (((1,), (1,)), ((), ()))
SMEM = pl.BlockSpec(memory_space=pltpu.SMEM)
VMEM = pl.BlockSpec(memory_space=pltpu.VMEM)
TOK, QUARTER, HALF, WINDOW, OFFSET = 512, 896, 448, 512, 384
DOCS, SLOTS, MEMBERS, SHARE = 128, 256, 512, 128


def params(mib=20):
    return pltpu.CompilerParams(vmem_limit_bytes=mib * 1024 * 1024)


def cost(flops, nbytes):
    return pl.CostEstimate(flops=flops, bytes_accessed=nbytes, transcendentals=0)


def device(z, y, core, x):
    return ((z * 8 + y) * 2 + core) * 4 + x


def placed(core, ring, line):
    return (ring, line) if core == 0 else (line, ring)


def grid():
    return [(z, y, c, x) for z in range(8) for y in range(8) for c in range(2) for x in range(4)]


def spread(flip):
    pairs = []
    for z, y, core, x in grid():
        to = core ^ flip
        to_z, to_y = placed(to, 2 * x + z % 2, y)
        pairs.append((device(z, y, core, x), device(to_z, to_y, to, z // 2)))
    return pairs


def groups(along):
    found = []
    for core in range(2):
        for x in range(4):
            for other in range(8):
                over_z = (along == "ring") == (core == 0)
                found.append(
                    [device(i, other, core, x) if over_z else device(other, i, core, x) for i in range(8)]
                )
    return found


def pair(value, turn):
    pairs = []
    for z, y, core, x in grid():
        pairs.append((device(z, y, core, x), device(z, y, core, x ^ (1 if core == turn else 3))))
    return lax.ppermute(value, ALL, pairs)


def core_swap(value):
    return lax.ppermute(value, ALL, [(at, at ^ 4) for at in range(512)])


def window(core):
    return pl.ds(pl.multiple_of(core * OFFSET, 128), WINDOW)


def pack_kernel(place, context, theirs, residual, small, near, side):
    core = place[2]
    for out in (near, side):
        out[0:TOK, :] = context[:, window(core)]
        out[TOK : 2 * TOK, :] = theirs[...]
    for out, row, target in ((near, 1024, 3), (near, 1280, 5), (side, 1024, 4)):
        start = place[target] * QUARTER
        out[row : row + 128, :] = residual[:, pl.ds(pl.multiple_of(start, 128), WINDOW)]
        out[row + 128 : row + 256, :] = residual[
            :, pl.ds(pl.multiple_of(start + OFFSET, 128), WINDOW)
        ]
    near[1536:1552, :] = small[...]
    side[1280:1296, :] = small[...]


def gather_kernel(place, context, theirs, residual, near, side, far, ctx, res):
    x = place[1]
    ctx[x, 0:TOK, :] = context[:, window(place[2])]
    ctx[x, TOK : 2 * TOK, :] = theirs[...]

    def put(at, value):
        res[pl.ds(pl.multiple_of(at * 128, 128), 128), :] = value

    put(x, residual[:, pl.ds(pl.multiple_of(x * QUARTER, 128), QUARTER)])
    for index, piece, row in ((3, near, 1024), (4, side, 1024), (5, far, 1280)):
        ctx[place[index]] = piece[0 : 2 * TOK, :]
        left, right = piece[row : row + 128, :], piece[row + 128 : row + 256, 128:512]
        put(place[index], jnp.concatenate([left, right], axis=1))


def sum_block(ctx, weight, total):
    step = pl.program_id(0)
    half = lax.rem(step, 2)
    product = lax.dot_general(ctx[0], weight[...], NT, preferred_element_type=F32)

    @pl.when(step < 2)
    def _():
        total[half] = product

    @pl.when(step >= 2)
    def _():
        total[half] += product


def whole(total, pack):
    rows = pl.ds(pack * 128, 128)
    return jnp.concatenate([total[0, rows, :], total[1, rows, :]], axis=1)


def other_kernel(ctx, weight, out, total):
    sum_block(ctx, weight, total)

    @pl.when(pl.program_id(0) == 7)
    def _():
        for pack in range(4):
            out[pl.ds(pack * 128, 128), :] = whole(total, pack).astype(BF)


def own_kernel(ctx, weight, res, out, total):
    sum_block(ctx, weight, total)

    @pl.when(pl.program_id(0) == 7)
    def _():
        for pack in range(4):
            rows = pl.ds(pack * 128, 128)
            out[rows, :] = whole(total, pack) + res[rows, :].astype(F32)


def rms_kernel(own, swapped, squares):
    squares[...] = jnp.zeros_like(squares)
    for pack in range(4):
        rows = pl.ds(pack * 128, 128)
        value = own[rows, :] + swapped[rows, :].astype(F32)
        sq = value * value
        part = sq[:, 0:128]
        for tile in range(1, 7):
            part = part + sq[:, tile * 128 : tile * 128 + 128]
        squares[pl.ds(pack, 1), :] = jnp.sum(part.T, axis=0, keepdims=True)


def pool_kernel(own, swapped, gain, pool, inverse, total, slots, squares):
    scale = lax.rsqrt(total[...] / 3584.0 + 1e-06)
    summed = None
    for pack in range(4):
        rows = pl.ds(pack * 128, 128)
        column = jnp.broadcast_to(scale[pack : pack + 1, :], (128, 128)).T
        column = jnp.concatenate([column] * 7, axis=1)
        hidden = own[rows, :] + swapped[rows, :].astype(F32)
        normed = (hidden * column * gain[...]).astype(BF)
        term = jnp.dot(pool[:, pack * 128 : pack * 128 + 128], normed, preferred_element_type=F32)
        summed = term if summed is None else summed + term
    pooled = summed * jnp.concatenate([inverse[...]] * 7, axis=1)
    slots[...] = pooled.astype(BF)
    sq = pooled * pooled
    part = sq[:, 0:128]
    for tile in range(1, 7):
        part = part + sq[:, tile * 128 : tile * 128 + 128]
    squares[...] = jnp.zeros_like(squares)
    for block in range(2):
        squares[pl.ds(block, 1), :] = jnp.sum(
            part[block * 128 : block * 128 + 128, :].T, axis=0, keepdims=True
        )


def dots_kernel(arrived, members, factor, out):
    for part in range(4):
        rows = pl.ds(part * SHARE, SHARE)
        dots = lax.dot_general(arrived[...], members[rows, :], NT, preferred_element_type=F32)
        out[:, part * SHARE : part * SHARE + SHARE] = (dots * factor[pl.ds(part, 1), :]).astype(BF)


def home_kernel(returned, pick, scale, live, scores, best):
    rows = jnp.dot(pick[...], returned[...], preferred_element_type=F32) * scale[...]
    scores[...] = rows
    masked = jnp.where(live[...] > 0.0, rows, -1000000000.0)
    best[...] = jnp.broadcast_to(jnp.max(masked.T, axis=0, keepdims=True), (8, 128))


def body(
    context,
    residual,
    out_weight,
    norm_gain,
    members,
    doc_lengths,
    doc_cluster,
    owner_map,
    member_counts,
):
    z, y = lax.axis_index("z"), lax.axis_index("y")
    core, x = lax.axis_index("core"), lax.axis_index("tensor")

    first = core == 0
    ring, line = jnp.where(first, z, y), jnp.where(first, y, z)
    near_x = jnp.where(first, x ^ 1, x ^ 3)
    side_x = jnp.where(first, x ^ 3, x ^ 1)
    far_x = x ^ 2
    place = jnp.stack([ring, x, core, near_x, side_x, far_x]).astype(jnp.int32)

    weight = out_weight.T
    lanes = lax.broadcasted_iota(jnp.int32, (28, WINDOW), 1)
    low = weight[:, :WINDOW]
    high = jnp.where(lanes < WINDOW - OFFSET, 0, weight[:, OFFSET:])
    keep = lax.ppermute(jnp.where(first, low, high), ALL, spread(0))
    cross = lax.ppermute(jnp.where(first, high, low), ALL, spread(1))
    block = jnp.concatenate(
        [jnp.where(first, keep, cross), jnp.where(first, cross, keep)], axis=0
    )

    late_context, _ = lax.optimization_barrier((context, keep))
    theirs = core_swap(jnp.where(first, late_context[:, OFFSET:], late_context[:, :WINDOW]))
    resident = members[0]
    resident_f = resident.astype(F32)
    partial_sq = jnp.sum(resident_f * resident_f, axis=-1).astype(BF)
    small = jnp.concatenate(
        [partial_sq.reshape(4, 128), jnp.pad(doc_lengths.astype(BF), ((0, 0), (0, 96)))], axis=0
    )
    small = jnp.pad(small, ((0, 11), (0, WINDOW - 128)))
    late_theirs, _ = lax.optimization_barrier((theirs, block))
    to_near, to_side = pl.pallas_call(
        pack_kernel,
        out_shape=(
            jax.ShapeDtypeStruct((1552, WINDOW), BF),
            jax.ShapeDtypeStruct((1296, WINDOW), BF),
        ),
        in_specs=[SMEM] + [pl.BlockSpec()] * 4,
        out_specs=(pl.BlockSpec(), pl.BlockSpec()),
        compiler_params=params(56),
        cost_estimate=cost(0, 6_000_000),
        name="pack",
    )(place, context, late_theirs, residual, small)
    block, to_near = lax.optimization_barrier((block, to_near))
    near = pair(to_near, 0)
    plane = lax.all_to_all(
        jnp.broadcast_to(block[None], (8, 56, WINDOW)), ALL, 0, 0,
        axis_index_groups=groups("line"), tiled=True,
    ).reshape(HALF, WINDOW)
    plane, near, to_side = lax.optimization_barrier((plane, near, to_side))
    plane = lax.all_gather(plane, ALL, axis=0, axis_index_groups=groups("ring"), tiled=True)
    far, side = pair(near, 1), pair(to_side, 1)

    tails = [(x, small), (near_x, near[-16:]), (side_x, side[-16:]), (far_x, far[-16:])]
    member_sq = sum((tail[:4, :128].astype(F32) for _, tail in tails[1:]), small[:4, :128].astype(F32))
    lens = jnp.zeros((4, 32), F32)
    for at, tail in tails:
        lens = lax.dynamic_update_slice(lens, tail[4:5, :32].astype(F32), (at, 0))

    cluster_ids = jnp.arange(owner_map.shape[0], dtype=jnp.int32)
    matches = doc_cluster[:, 0][:, None] == cluster_ids[None, :]
    doc_owner = jnp.sum(jnp.where(matches, owner_map[None, :], 0), axis=1)
    doc_members = jnp.sum(jnp.where(matches, member_counts[None, :], 0), axis=1)
    doc_order = jnp.arange(DOCS, dtype=jnp.int32)
    same_owner = (doc_owner[:, None] == doc_owner[None, :]) & (
        doc_order[:, None] > doc_order[None, :]
    )
    doc_slot = doc_owner * 2 + jnp.sum(same_owner.astype(jnp.int32), axis=1)
    slot_ids = jnp.arange(SLOTS, dtype=jnp.int32)
    select = slot_ids[:, None] == doc_slot[None, :]
    wide_ids = jnp.arange(4 * SLOTS, dtype=jnp.int32)
    wide_ids = lax.div(wide_ids, 8) * 2 + lax.rem(wide_ids, 2)
    pick = (doc_slot[:, None] == wide_ids[None, :]).astype(BF)
    lens_int = lens.astype(jnp.int32)
    ends = jnp.cumsum(lens_int, axis=1)
    offsets = 128 * jnp.arange(4, dtype=jnp.int32)[:, None]
    doc_begin = (ends - lens_int + offsets).reshape(DOCS)
    doc_end = (ends + offsets).reshape(DOCS)
    tokens = jnp.arange(TOK, dtype=jnp.int32)
    inside = (tokens[None, :] >= doc_begin[:, None]) & (tokens[None, :] < doc_end[:, None])
    pool = jnp.dot(select.astype(BF), inside.astype(BF), preferred_element_type=F32).astype(BF)
    slot_len = jnp.sum(jnp.where(select, lens.reshape(DOCS)[None, :], 0.0), axis=1)
    inverse = jnp.broadcast_to((1.0 / jnp.maximum(slot_len, 1.0))[:, None], (SLOTS, 128))
    columns = x * SHARE + jnp.arange(SHARE, dtype=jnp.int32)
    live = (columns[None, :] < doc_members[:, None]).astype(F32)

    own_dp = (z * 8 + y) * 2 + core
    own_count = jnp.sum(jnp.where(owner_map == own_dp, member_counts, 0))
    member_ids = jnp.arange(MEMBERS, dtype=jnp.int32).reshape(4, 128)
    factor = jnp.where(member_ids < own_count, lax.rsqrt(member_sq / 3584.0 + 1e-06), 0.0)

    ctx, res = pl.pallas_call(
        gather_kernel,
        out_shape=(
            jax.ShapeDtypeStruct((4, 2 * TOK, WINDOW), BF),
            jax.ShapeDtypeStruct((TOK, QUARTER), BF),
        ),
        in_specs=[SMEM] + [pl.BlockSpec()] * 6,
        out_specs=(pl.BlockSpec(), pl.BlockSpec()),
        compiler_params=params(56),
        cost_estimate=cost(0, 10_000_000),
        name="gather",
    )(place, context, theirs, residual, near, side, far)
    weight_spec = pl.BlockSpec((HALF, WINDOW), lambda i: (i, 0))
    out_spec = pl.BlockSpec((TOK, QUARTER), lambda i: (0, 0))
    half_cost = cost(8 * 2 * TOK * WINDOW * HALF, 8_000_000)
    other = pl.pallas_call(
        other_kernel,
        out_shape=jax.ShapeDtypeStruct((TOK, QUARTER), BF),
        grid=(8,),
        in_specs=[pl.BlockSpec((1, TOK, WINDOW), lambda i: (lax.div(i, 2), 1, 0)), weight_spec],
        out_specs=out_spec,
        scratch_shapes=[pltpu.VMEM((2, TOK, HALF), F32)],
        compiler_params=params(56),
        cost_estimate=half_cost,
        name="other",
    )(ctx, plane)
    swapped = core_swap(other)
    own = pl.pallas_call(
        own_kernel,
        out_shape=jax.ShapeDtypeStruct((TOK, QUARTER), F32),
        grid=(8,),
        in_specs=[
            pl.BlockSpec((1, TOK, WINDOW), lambda i: (lax.div(i, 2), 0, 0)),
            weight_spec,
            out_spec,
        ],
        out_specs=out_spec,
        scratch_shapes=[pltpu.VMEM((2, TOK, HALF), F32)],
        compiler_params=params(56),
        cost_estimate=half_cost,
        name="own",
    )(ctx, plane, res)
    squares = pl.pallas_call(
        rms_kernel,
        out_shape=jax.ShapeDtypeStruct((8, 128), F32),
        in_specs=[VMEM] * 2,
        out_specs=VMEM,
        compiler_params=params(),
        cost_estimate=cost(2 * TOK * QUARTER, 3_000_000),
        name="rms",
    )(own, swapped)

    slots, doc_sq = pl.pallas_call(
        pool_kernel,
        out_shape=(
            jax.ShapeDtypeStruct((SLOTS, QUARTER), BF),
            jax.ShapeDtypeStruct((8, 128), F32),
        ),
        in_specs=[VMEM] * 6,
        out_specs=(VMEM, VMEM),
        compiler_params=params(),
        cost_estimate=cost(2 * SLOTS * TOK * QUARTER, 3_000_000),
        name="pool",
    )(own, swapped, gain_of(norm_gain, x), pool, inverse, lax.psum(squares, "tensor"))

    arrived = lax.all_to_all(
        slots.reshape(DOCS, 2, QUARTER), DP, split_axis=0, concat_axis=0, tiled=True
    ).reshape(SLOTS, QUARTER)

    slot_sq = lax.psum(doc_sq, "tensor")[:2].reshape(SLOTS)
    doc_total = jnp.sum(jnp.where(select, slot_sq[:, None], 0.0), axis=0)
    scale = jnp.broadcast_to(lax.rsqrt(doc_total + 1e-06)[:, None], (DOCS, SHARE))

    partial = pl.pallas_call(
        dots_kernel,
        out_shape=jax.ShapeDtypeStruct((SLOTS, MEMBERS), BF),
        in_specs=[VMEM] * 3,
        out_specs=VMEM,
        compiler_params=params(),
        cost_estimate=cost(2 * SLOTS * MEMBERS * QUARTER, 2_000_000),
        name="dots",
    )(arrived, resident, factor)

    partial = partial.reshape(DOCS, 2, 4, SHARE).transpose(0, 2, 1, 3).reshape(4 * DOCS, 2, SHARE)
    returned = lax.all_to_all(partial, ALL, split_axis=0, concat_axis=0, tiled=True)
    returned = returned.reshape(4 * SLOTS, SHARE)
    scores, best = pl.pallas_call(
        home_kernel,
        out_shape=(
            jax.ShapeDtypeStruct((DOCS, SHARE), F32),
            jax.ShapeDtypeStruct((8, 128), F32),
        ),
        in_specs=[VMEM] * 4,
        out_specs=(VMEM, VMEM),
        compiler_params=params(),
        cost_estimate=cost(2 * SLOTS * DOCS * SHARE, 400_000),
        name="home",
    )(returned, pick, scale, live)
    return scores, lax.pmax(best[0], "tensor")


def gain_of(norm_gain, x):
    return lax.dynamic_slice(norm_gain, (x * QUARTER,), (QUARTER,)).reshape(1, QUARTER)


def solution(mesh):
    split = Mesh(mesh.devices.reshape(8, 8, 2, 4), ALL)
    in_specs = (
        P(DP, "tensor"),
        P(ALL, None),
        P("tensor", DP),
        P(),
        P(DP, None, "tensor"),
        P(ALL, None),
        P(DP, None),
        P(),
        P(),
    )
    out_specs = (P(DP, "tensor"), P(DP))
    return jax.shard_map(body, mesh=split, in_specs=in_specs, out_specs=out_specs, check_vma=False)
```

```python
import jax
import jax.numpy as jnp
from jax import lax
from jax.experimental import pallas as pl
from jax.experimental.pallas import tpu as pltpu
from jax.sharding import Mesh, PartitionSpec as P

DP = ("z", "y", "core")
ALL = ("z", "y", "core", "tensor")
BF = jnp.bfloat16
F32 = jnp.float32
NT = (((1,), (1,)), ((), ()))
SMEM = pl.BlockSpec(memory_space=pltpu.SMEM)
VMEM = pl.BlockSpec(memory_space=pltpu.VMEM)
TOK, QUARTER, HALF = 512, 896, 448
DOCS, SLOTS, MEMBERS, SHARE = 128, 256, 512, 128


def params(mib=20):
    return pltpu.CompilerParams(vmem_limit_bytes=mib * 1024 * 1024)


def cost(flops, nbytes):
    return pl.CostEstimate(flops=flops, bytes_accessed=nbytes, transcendentals=0)


def device(z, y, core, x):
    return ((z * 8 + y) * 2 + core) * 4 + x


def placed(core, ring, line):
    return (ring, line) if core == 0 else (line, ring)


def grid():
    return [(z, y, c, x) for z in range(8) for y in range(8) for c in range(2) for x in range(4)]


def spread(flip):
    pairs = []
    for z, y, core, x in grid():
        to = core ^ flip
        to_z, to_y = placed(to, 2 * x + z % 2, y)
        pairs.append((device(z, y, core, x), device(to_z, to_y, to, z // 2)))
    return pairs


def groups(along):
    found = []
    for core in range(2):
        for x in range(4):
            for other in range(8):
                over_z = (along == "ring") == (core == 0)
                found.append(
                    [device(i, other, core, x) if over_z else device(other, i, core, x) for i in range(8)]
                )
    return found


def pair(value, turn):
    pairs = []
    for z, y, core, x in grid():
        pairs.append((device(z, y, core, x), device(z, y, core, x ^ (1 if core == turn else 3))))
    return lax.ppermute(value, ALL, pairs)


def core_swap(value):
    return lax.ppermute(value, ALL, [(at, at ^ 4) for at in range(512)])


def pack_kernel(place, context, residual, small, near, side):
    near[0:TOK, :] = context[...]
    side[0:TOK, :] = context[...]
    for out, row, target in ((near, 512, 1), (near, 640, 3), (side, 512, 2)):
        start = pl.multiple_of(place[target] * QUARTER, 128)
        out[row : row + 128, :] = residual[:, pl.ds(start, QUARTER)]
    near[768:784, :] = small[...]
    side[640:656, :] = small[...]


def project_kernel(place, context, near, side, far, weight, res, hidden, squares):
    step = pl.program_id(0)
    for index, piece in enumerate((context, near, side, far)):

        @pl.when(step == index)
        def _(index=index, piece=piece):
            product = lax.dot_general(piece[0:TOK, :], weight[...], NT, preferred_element_type=F32)
            if index == 0:
                hidden[...] = product
            else:
                hidden[...] += product

    @pl.when(step == 3)
    def _():
        tails = (res[...], near[512:640, :], side[512:640, :], far[640:768, :])
        for index, tail in enumerate(tails):
            rows = pl.ds(pl.multiple_of(place[index] * 128, 128), 128)
            hidden[rows, :] += tail.astype(F32)
        squares[...] = jnp.zeros_like(squares)
        for pack in range(4):
            value = hidden[pl.ds(pack * 128, 128), :]
            sq = value * value
            part = sq[:, 0:128]
            for tile in range(1, 7):
                part = part + sq[:, tile * 128 : tile * 128 + 128]
            squares[pl.ds(pack, 1), :] = jnp.sum(part.T, axis=0, keepdims=True)


def pool_kernel(hidden, gain, pool, inverse, total, slots, squares):
    scale = lax.rsqrt(total[...] / 3584.0 + 1e-06)
    summed = None
    for pack in range(4):
        rows = pl.ds(pack * 128, 128)
        column = jnp.broadcast_to(scale[pack : pack + 1, :], (128, 128)).T
        column = jnp.concatenate([column] * 7, axis=1)
        normed = (hidden[rows, :] * column * gain[...]).astype(BF)
        term = jnp.dot(pool[:, pack * 128 : pack * 128 + 128], normed, preferred_element_type=F32)
        summed = term if summed is None else summed + term
    pooled = summed * jnp.concatenate([inverse[...]] * 7, axis=1)
    slots[...] = pooled.astype(BF)
    sq = pooled * pooled
    part = sq[:, 0:128]
    for tile in range(1, 7):
        part = part + sq[:, tile * 128 : tile * 128 + 128]
    squares[...] = jnp.zeros_like(squares)
    for block in range(2):
        squares[pl.ds(block, 1), :] = jnp.sum(
            part[block * 128 : block * 128 + 128, :].T, axis=0, keepdims=True
        )


def dots_kernel(arrived, members, factor, out):
    for part in range(4):
        rows = pl.ds(part * SHARE, SHARE)
        dots = lax.dot_general(arrived[...], members[rows, :], NT, preferred_element_type=F32)
        out[:, part * SHARE : part * SHARE + SHARE] = (dots * factor[pl.ds(part, 1), :]).astype(BF)


def home_kernel(returned, pick, scale, live, scores, best):
    rows = jnp.dot(pick[...], returned[...], preferred_element_type=F32) * scale[...]
    scores[...] = rows
    masked = jnp.where(live[...] > 0.0, rows, -1000000000.0)
    best[...] = jnp.broadcast_to(jnp.max(masked.T, axis=0, keepdims=True), (8, 128))


def body(
    context,
    residual,
    out_weight,
    norm_gain,
    members,
    doc_lengths,
    doc_cluster,
    owner_map,
    member_counts,
):
    z, y = lax.axis_index("z"), lax.axis_index("y")
    core, x = lax.axis_index("core"), lax.axis_index("tensor")

    first = core == 0
    near_x = jnp.where(first, x ^ 1, x ^ 3)
    side_x = jnp.where(first, x ^ 3, x ^ 1)
    far_x = x ^ 2
    place = jnp.stack([x, near_x, side_x, far_x]).astype(jnp.int32)

    weight = out_weight.T
    keep = lax.ppermute(weight, ALL, spread(0))
    cross = lax.ppermute(weight, ALL, spread(1))
    block = jnp.concatenate(
        [jnp.where(first, keep, cross), jnp.where(first, cross, keep)], axis=0
    )

    resident = members[0]
    resident_f = resident.astype(F32)
    partial_sq = jnp.sum(resident_f * resident_f, axis=-1).astype(BF)
    small = jnp.concatenate(
        [partial_sq.reshape(4, 128), jnp.pad(doc_lengths.astype(BF), ((0, 0), (0, 96)))], axis=0
    )
    small = jnp.pad(small, ((0, 11), (0, QUARTER - 128)))
    to_near, to_side = pl.pallas_call(
        pack_kernel,
        out_shape=(
            jax.ShapeDtypeStruct((784, QUARTER), BF),
            jax.ShapeDtypeStruct((656, QUARTER), BF),
        ),
        in_specs=[SMEM] + [pl.BlockSpec()] * 3,
        out_specs=(pl.BlockSpec(), pl.BlockSpec()),
        compiler_params=params(56),
        cost_estimate=cost(0, 6_000_000),
        name="pack",
    )(place, context, residual, small)

    block, to_near = lax.optimization_barrier((block, to_near))
    near = pair(to_near, 0)
    plane = lax.all_to_all(
        jnp.broadcast_to(block[None], (8, 56, QUARTER)), ALL, 0, 0,
        axis_index_groups=groups("line"), tiled=True,
    ).reshape(HALF, QUARTER)
    plane, near, to_side = lax.optimization_barrier((plane, near, to_side))
    plane = lax.all_gather(plane, ALL, axis=0, axis_index_groups=groups("ring"), tiled=True)
    far, side = pair(near, 1), pair(to_side, 1)

    tails = [(x, small), (near_x, near[-16:]), (side_x, side[-16:]), (far_x, far[-16:])]
    member_sq = sum((tail[:4, :128].astype(F32) for _, tail in tails[1:]), small[:4, :128].astype(F32))
    lens = jnp.zeros((4, 32), F32)
    for at, tail in tails:
        lens = lax.dynamic_update_slice(lens, tail[4:5, :32].astype(F32), (at, 0))

    cluster_ids = jnp.arange(owner_map.shape[0], dtype=jnp.int32)
    matches = doc_cluster[:, 0][:, None] == cluster_ids[None, :]
    doc_owner = jnp.sum(jnp.where(matches, owner_map[None, :], 0), axis=1)
    doc_members = jnp.sum(jnp.where(matches, member_counts[None, :], 0), axis=1)
    doc_order = jnp.arange(DOCS, dtype=jnp.int32)
    same_owner = (doc_owner[:, None] == doc_owner[None, :]) & (
        doc_order[:, None] > doc_order[None, :]
    )
    doc_slot = doc_owner * 2 + jnp.sum(same_owner.astype(jnp.int32), axis=1)
    slot_ids = jnp.arange(SLOTS, dtype=jnp.int32)
    select = slot_ids[:, None] == doc_slot[None, :]
    wide_ids = jnp.arange(4 * SLOTS, dtype=jnp.int32)
    wide_ids = lax.div(wide_ids, 8) * 2 + lax.rem(wide_ids, 2)
    pick = (doc_slot[:, None] == wide_ids[None, :]).astype(BF)
    lens_int = lens.astype(jnp.int32)
    ends = jnp.cumsum(lens_int, axis=1)
    offsets = 128 * jnp.arange(4, dtype=jnp.int32)[:, None]
    doc_begin = (ends - lens_int + offsets).reshape(DOCS)
    doc_end = (ends + offsets).reshape(DOCS)
    tokens = jnp.arange(TOK, dtype=jnp.int32)
    inside = (tokens[None, :] >= doc_begin[:, None]) & (tokens[None, :] < doc_end[:, None])
    pool = jnp.dot(select.astype(BF), inside.astype(BF), preferred_element_type=F32).astype(BF)
    slot_len = jnp.sum(jnp.where(select, lens.reshape(DOCS)[None, :], 0.0), axis=1)
    inverse = jnp.broadcast_to((1.0 / jnp.maximum(slot_len, 1.0))[:, None], (SLOTS, 128))
    columns = x * SHARE + jnp.arange(SHARE, dtype=jnp.int32)
    live = (columns[None, :] < doc_members[:, None]).astype(F32)

    own_dp = (z * 8 + y) * 2 + core
    own_count = jnp.sum(jnp.where(owner_map == own_dp, member_counts, 0))
    member_ids = jnp.arange(MEMBERS, dtype=jnp.int32).reshape(4, 128)
    factor = jnp.where(member_ids < own_count, lax.rsqrt(member_sq / 3584.0 + 1e-06), 0.0)

    res = lax.dynamic_slice(residual, (0, x * QUARTER), (128, QUARTER))
    hidden, squares = pl.pallas_call(
        project_kernel,
        out_shape=(
            jax.ShapeDtypeStruct((TOK, QUARTER), F32),
            jax.ShapeDtypeStruct((8, 128), F32),
        ),
        grid_spec=pltpu.PrefetchScalarGridSpec(
            num_scalar_prefetch=1,
            grid=(4,),
            in_specs=[
                pl.BlockSpec((TOK, QUARTER), lambda i, place: (0, 0)),
                pl.BlockSpec((784, QUARTER), lambda i, place: (0, 0)),
                pl.BlockSpec((656, QUARTER), lambda i, place: (0, 0)),
                pl.BlockSpec((784, QUARTER), lambda i, place: (0, 0)),
                pl.BlockSpec((QUARTER, QUARTER), lambda i, place: (place[i], 0)),
                pl.BlockSpec((128, QUARTER), lambda i, place: (0, 0)),
            ],
            out_specs=(
                pl.BlockSpec((TOK, QUARTER), lambda i, place: (0, 0)),
                pl.BlockSpec((8, 128), lambda i, place: (0, 0)),
            ),
        ),
        compiler_params=params(56),
        cost_estimate=cost(2 * TOK * QUARTER * 3584, 13_000_000),
        name="project",
    )(place, context, near, side, far, plane, res)

    slots, doc_sq = pl.pallas_call(
        pool_kernel,
        out_shape=(
            jax.ShapeDtypeStruct((SLOTS, QUARTER), BF),
            jax.ShapeDtypeStruct((8, 128), F32),
        ),
        in_specs=[VMEM] * 5,
        out_specs=(VMEM, VMEM),
        compiler_params=params(),
        cost_estimate=cost(2 * SLOTS * TOK * QUARTER, 3_000_000),
        name="pool",
    )(hidden, gain_of(norm_gain, x), pool, inverse, lax.psum(squares, "tensor"))

    arrived = lax.all_to_all(
        slots.reshape(DOCS, 2, QUARTER), DP, split_axis=0, concat_axis=0, tiled=True
    ).reshape(SLOTS, QUARTER)

    slot_sq = lax.psum(doc_sq, "tensor")[:2].reshape(SLOTS)
    doc_total = jnp.sum(jnp.where(select, slot_sq[:, None], 0.0), axis=0)
    scale = jnp.broadcast_to(lax.rsqrt(doc_total + 1e-06)[:, None], (DOCS, SHARE))

    partial = pl.pallas_call(
        dots_kernel,
        out_shape=jax.ShapeDtypeStruct((SLOTS, MEMBERS), BF),
        in_specs=[VMEM] * 3,
        out_specs=VMEM,
        compiler_params=params(),
        cost_estimate=cost(2 * SLOTS * MEMBERS * QUARTER, 2_000_000),
        name="dots",
    )(arrived, resident, factor)

    partial = partial.reshape(DOCS, 2, 4, SHARE).transpose(0, 2, 1, 3).reshape(4 * DOCS, 2, SHARE)
    returned = lax.all_to_all(partial, ALL, split_axis=0, concat_axis=0, tiled=True)
    returned = returned.reshape(4 * SLOTS, SHARE)
    scores, best = pl.pallas_call(
        home_kernel,
        out_shape=(
            jax.ShapeDtypeStruct((DOCS, SHARE), F32),
            jax.ShapeDtypeStruct((8, 128), F32),
        ),
        in_specs=[VMEM] * 4,
        out_specs=(VMEM, VMEM),
        compiler_params=params(),
        cost_estimate=cost(2 * SLOTS * DOCS * SHARE, 400_000),
        name="home",
    )(returned, pick, scale, live)
    return scores, lax.pmax(best[0], "tensor")


def gain_of(norm_gain, x):
    return lax.dynamic_slice(norm_gain, (x * QUARTER,), (QUARTER,)).reshape(1, QUARTER)


def solution(mesh):
    split = Mesh(mesh.devices.reshape(8, 8, 2, 4), ALL)
    in_specs = (
        P(DP, "tensor"),
        P(ALL, None),
        P("tensor", DP),
        P(),
        P(DP, None, "tensor"),
        P(ALL, None),
        P(DP, None),
        P(),
        P(),
    )
    out_specs = (P(DP, "tensor"), P(DP))
    return jax.shard_map(body, mesh=split, in_specs=in_specs, out_specs=out_specs, check_vma=False)
```

```python
import jax
import jax.numpy as jnp
from jax import lax
from jax.experimental import pallas as pl
from jax.experimental.pallas import tpu as pltpu
from jax.sharding import Mesh, PartitionSpec as P

DP = ("z", "y", "core")
ALL = ("z", "y", "core", "tensor")
BF = jnp.bfloat16
F32 = jnp.float32
NT = (((1,), (1,)), ((), ()))
SMEM = pl.BlockSpec(memory_space=pltpu.SMEM)
VMEM = pl.BlockSpec(memory_space=pltpu.VMEM)
TOK, QUARTER, HALF = 512, 896, 448
DOCS, SLOTS, MEMBERS, SHARE = 128, 256, 512, 128


def params(mib=20):
    return pltpu.CompilerParams(vmem_limit_bytes=mib * 1024 * 1024)


def cost(flops, nbytes):
    return pl.CostEstimate(flops=flops, bytes_accessed=nbytes, transcendentals=0)


def device(z, y, core, x):
    return ((z * 8 + y) * 2 + core) * 4 + x


def placed(core, ring, line):
    return (ring, line) if core == 0 else (line, ring)


def grid():
    return [(z, y, c, x) for z in range(8) for y in range(8) for c in range(2) for x in range(4)]


def spread(flip):
    pairs = []
    for z, y, core, x in grid():
        to = core ^ flip
        to_z, to_y = placed(to, 2 * x + z % 2, y)
        pairs.append((device(z, y, core, x), device(to_z, to_y, to, z // 2)))
    return pairs


def groups(along):
    found = []
    for core in range(2):
        for x in range(4):
            for other in range(8):
                over_z = (along == "ring") == (core == 0)
                found.append(
                    [device(i, other, core, x) if over_z else device(other, i, core, x) for i in range(8)]
                )
    return found


def pair(value, turn):
    pairs = []
    for z, y, core, x in grid():
        pairs.append((device(z, y, core, x), device(z, y, core, x ^ (1 if core == turn else 3))))
    return lax.ppermute(value, ALL, pairs)


def core_swap(value):
    return lax.ppermute(value, ALL, [(at, at ^ 4) for at in range(512)])


def pack_kernel(place, context, residual, small, near, side):
    near[0:TOK, :] = context[...]
    side[0:TOK, :] = context[...]
    for out, row, target in ((near, 512, 1), (near, 640, 3), (side, 512, 2)):
        start = pl.multiple_of(place[target] * QUARTER, 128)
        out[row : row + 128, :] = residual[:, pl.ds(start, QUARTER)]
    near[768:784, :] = small[...]
    side[640:656, :] = small[...]


def project_kernel(
    place, context, near, side, far, weight, res, hidden, squares, ctx, tails, blocks, sems
):
    def fetch(source, target, at):
        return pltpu.make_async_copy(source, target, sems.at[at])

    copies = []
    for index, piece in enumerate((context, near, side, far)):
        start = pl.multiple_of(place[index] * QUARTER, QUARTER)
        copies.append(
            (
                fetch(piece.at[pl.ds(0, TOK), :], ctx.at[index], 2 * index),
                fetch(weight.at[pl.ds(start, QUARTER), :], blocks.at[index], 2 * index + 1),
            )
        )
    ends = [
        fetch(piece.at[pl.ds(row, 128), :], tails.at[index], 8 + index)
        for index, (piece, row) in enumerate(((res, 0), (near, 512), (side, 512), (far, 640)))
    ]
    for pair_of in copies:
        for copy in pair_of:
            copy.start()
    for copy in ends:
        copy.start()
    for index in range(4):
        for copy in copies[index]:
            copy.wait()
        product = lax.dot_general(ctx[index], blocks[index], NT, preferred_element_type=F32)
        if index == 0:
            hidden[...] = product
        else:
            hidden[...] += product
    for copy in ends:
        copy.wait()
    squares[...] = jnp.zeros_like(squares)
    for index in range(4):
        at = place[index]
        rows = pl.ds(pl.multiple_of(at * 128, 128), 128)
        value = hidden[rows, :] + tails[index].astype(F32)
        hidden[rows, :] = value
        sq = value * value
        part = sq[:, 0:128]
        for tile in range(1, 7):
            part = part + sq[:, tile * 128 : tile * 128 + 128]
        squares[pl.ds(at, 1), :] = jnp.sum(part.T, axis=0, keepdims=True)


def pool_kernel(hidden, gain, pool, inverse, total, slots, squares):
    scale = lax.rsqrt(total[...] / 3584.0 + 1e-06)
    summed = None
    for pack in range(4):
        rows = pl.ds(pack * 128, 128)
        column = jnp.broadcast_to(scale[pack : pack + 1, :], (128, 128)).T
        column = jnp.concatenate([column] * 7, axis=1)
        normed = (hidden[rows, :] * column * gain[...]).astype(BF)
        term = jnp.dot(pool[:, pack * 128 : pack * 128 + 128], normed, preferred_element_type=F32)
        summed = term if summed is None else summed + term
    pooled = summed * jnp.concatenate([inverse[...]] * 7, axis=1)
    slots[...] = pooled.astype(BF)
    sq = pooled * pooled
    part = sq[:, 0:128]
    for tile in range(1, 7):
        part = part + sq[:, tile * 128 : tile * 128 + 128]
    squares[...] = jnp.zeros_like(squares)
    for block in range(2):
        squares[pl.ds(block, 1), :] = jnp.sum(
            part[block * 128 : block * 128 + 128, :].T, axis=0, keepdims=True
        )


def dots_kernel(arrived, members, factor, out):
    for part in range(4):
        rows = pl.ds(part * SHARE, SHARE)
        dots = lax.dot_general(arrived[...], members[rows, :], NT, preferred_element_type=F32)
        out[:, part * SHARE : part * SHARE + SHARE] = (dots * factor[pl.ds(part, 1), :]).astype(BF)


def home_kernel(returned, pick, scale, live, scores, best):
    rows = jnp.dot(pick[...], returned[...], preferred_element_type=F32) * scale[...]
    scores[...] = rows
    masked = jnp.where(live[...] > 0.0, rows, -1000000000.0)
    best[...] = jnp.broadcast_to(jnp.max(masked.T, axis=0, keepdims=True), (8, 128))


def body(
    context,
    residual,
    out_weight,
    norm_gain,
    members,
    doc_lengths,
    doc_cluster,
    owner_map,
    member_counts,
):
    z, y = lax.axis_index("z"), lax.axis_index("y")
    core, x = lax.axis_index("core"), lax.axis_index("tensor")

    first = core == 0
    near_x = jnp.where(first, x ^ 1, x ^ 3)
    side_x = jnp.where(first, x ^ 3, x ^ 1)
    far_x = x ^ 2
    place = jnp.stack([x, near_x, side_x, far_x]).astype(jnp.int32)

    weight = out_weight.T
    keep = lax.ppermute(weight, ALL, spread(0))
    cross = lax.ppermute(weight, ALL, spread(1))
    block = jnp.concatenate(
        [jnp.where(first, keep, cross), jnp.where(first, cross, keep)], axis=0
    )

    resident = members[0]
    resident_f = resident.astype(F32)
    partial_sq = jnp.sum(resident_f * resident_f, axis=-1).astype(BF)
    small = jnp.concatenate(
        [partial_sq.reshape(4, 128), jnp.pad(doc_lengths.astype(BF), ((0, 0), (0, 96)))], axis=0
    )
    small = jnp.pad(small, ((0, 11), (0, QUARTER - 128)))
    to_near, to_side = pl.pallas_call(
        pack_kernel,
        out_shape=(
            jax.ShapeDtypeStruct((784, QUARTER), BF),
            jax.ShapeDtypeStruct((656, QUARTER), BF),
        ),
        in_specs=[SMEM] + [VMEM] * 3,
        out_specs=(pl.BlockSpec(), pl.BlockSpec()),
        compiler_params=params(),
        cost_estimate=cost(0, 6_000_000),
        name="pack",
    )(place, context, residual, small)

    near, side = pair(to_near, 0), pair(to_side, 1)
    plane = lax.all_to_all(
        jnp.broadcast_to(block[None], (8, 56, QUARTER)), ALL, 0, 0,
        axis_index_groups=groups("line"), tiled=True,
    ).reshape(HALF, QUARTER)
    plane, _, _ = lax.optimization_barrier((plane, to_near, to_side))
    plane = lax.all_gather(plane, ALL, axis=0, axis_index_groups=groups("ring"), tiled=True)
    far = pair(near, 1)

    tails = [(x, small), (near_x, near[-16:]), (side_x, side[-16:]), (far_x, far[-16:])]
    member_sq = sum((tail[:4, :128].astype(F32) for _, tail in tails[1:]), small[:4, :128].astype(F32))
    lens = jnp.zeros((4, 32), F32)
    for at, tail in tails:
        lens = lax.dynamic_update_slice(lens, tail[4:5, :32].astype(F32), (at, 0))

    cluster_ids = jnp.arange(owner_map.shape[0], dtype=jnp.int32)
    matches = doc_cluster[:, 0][:, None] == cluster_ids[None, :]
    doc_owner = jnp.sum(jnp.where(matches, owner_map[None, :], 0), axis=1)
    doc_members = jnp.sum(jnp.where(matches, member_counts[None, :], 0), axis=1)
    doc_order = jnp.arange(DOCS, dtype=jnp.int32)
    same_owner = (doc_owner[:, None] == doc_owner[None, :]) & (
        doc_order[:, None] > doc_order[None, :]
    )
    doc_slot = doc_owner * 2 + jnp.sum(same_owner.astype(jnp.int32), axis=1)
    slot_ids = jnp.arange(SLOTS, dtype=jnp.int32)
    select = slot_ids[:, None] == doc_slot[None, :]
    wide_ids = jnp.arange(4 * SLOTS, dtype=jnp.int32)
    wide_ids = lax.div(wide_ids, 8) * 2 + lax.rem(wide_ids, 2)
    pick = (doc_slot[:, None] == wide_ids[None, :]).astype(BF)
    lens_int = lens.astype(jnp.int32)
    ends = jnp.cumsum(lens_int, axis=1)
    offsets = 128 * jnp.arange(4, dtype=jnp.int32)[:, None]
    doc_begin = (ends - lens_int + offsets).reshape(DOCS)
    doc_end = (ends + offsets).reshape(DOCS)
    tokens = jnp.arange(TOK, dtype=jnp.int32)
    inside = (tokens[None, :] >= doc_begin[:, None]) & (tokens[None, :] < doc_end[:, None])
    pool = jnp.dot(select.astype(BF), inside.astype(BF), preferred_element_type=F32).astype(BF)
    slot_len = jnp.sum(jnp.where(select, lens.reshape(DOCS)[None, :], 0.0), axis=1)
    inverse = jnp.broadcast_to((1.0 / jnp.maximum(slot_len, 1.0))[:, None], (SLOTS, 128))
    columns = x * SHARE + jnp.arange(SHARE, dtype=jnp.int32)
    live = (columns[None, :] < doc_members[:, None]).astype(F32)

    own_dp = (z * 8 + y) * 2 + core
    own_count = jnp.sum(jnp.where(owner_map == own_dp, member_counts, 0))
    member_ids = jnp.arange(MEMBERS, dtype=jnp.int32).reshape(4, 128)
    factor = jnp.where(member_ids < own_count, lax.rsqrt(member_sq / 3584.0 + 1e-06), 0.0)

    res = lax.dynamic_slice(residual, (0, x * QUARTER), (128, QUARTER))
    hidden, squares = pl.pallas_call(
        project_kernel,
        out_shape=(
            jax.ShapeDtypeStruct((TOK, QUARTER), F32),
            jax.ShapeDtypeStruct((8, 128), F32),
        ),
        in_specs=[SMEM] + [pl.BlockSpec(memory_space=pl.ANY)] * 6,
        out_specs=(VMEM, VMEM),
        scratch_shapes=[
            pltpu.VMEM((4, TOK, QUARTER), BF),
            pltpu.VMEM((4, 128, QUARTER), BF),
            pltpu.VMEM((4, QUARTER, QUARTER), BF),
            pltpu.SemaphoreType.DMA((12,)),
        ],
        compiler_params=params(54),
        cost_estimate=cost(2 * TOK * QUARTER * 3584, 13_000_000),
        name="project",
    )(place, context, near, side, far, plane, res)

    slots, doc_sq = pl.pallas_call(
        pool_kernel,
        out_shape=(
            jax.ShapeDtypeStruct((SLOTS, QUARTER), BF),
            jax.ShapeDtypeStruct((8, 128), F32),
        ),
        in_specs=[VMEM] * 5,
        out_specs=(VMEM, VMEM),
        compiler_params=params(54),
        cost_estimate=cost(2 * SLOTS * TOK * QUARTER, 3_000_000),
        name="pool",
    )(hidden, gain_of(norm_gain, x), pool, inverse, lax.psum(squares, "tensor"))

    arrived = lax.all_to_all(
        slots.reshape(DOCS, 2, QUARTER), DP, split_axis=0, concat_axis=0, tiled=True
    ).reshape(SLOTS, QUARTER)

    slot_sq = lax.psum(doc_sq, "tensor")[:2].reshape(SLOTS)
    doc_total = jnp.sum(jnp.where(select, slot_sq[:, None], 0.0), axis=0)
    scale = jnp.broadcast_to(lax.rsqrt(doc_total + 1e-06)[:, None], (DOCS, SHARE))

    partial = pl.pallas_call(
        dots_kernel,
        out_shape=jax.ShapeDtypeStruct((SLOTS, MEMBERS), BF),
        in_specs=[VMEM] * 3,
        out_specs=VMEM,
        compiler_params=params(),
        cost_estimate=cost(2 * SLOTS * MEMBERS * QUARTER, 2_000_000),
        name="dots",
    )(arrived, resident, factor)

    partial = partial.reshape(DOCS, 2, 4, SHARE).transpose(0, 2, 1, 3).reshape(4 * DOCS, 2, SHARE)
    returned = lax.all_to_all(partial, ALL, split_axis=0, concat_axis=0, tiled=True)
    returned = returned.reshape(4 * SLOTS, SHARE)
    scores, best = pl.pallas_call(
        home_kernel,
        out_shape=(
            jax.ShapeDtypeStruct((DOCS, SHARE), F32),
            jax.ShapeDtypeStruct((8, 128), F32),
        ),
        in_specs=[VMEM] * 4,
        out_specs=(VMEM, VMEM),
        compiler_params=params(),
        cost_estimate=cost(2 * SLOTS * DOCS * SHARE, 400_000),
        name="home",
    )(returned, pick, scale, live)
    return scores, lax.pmax(best[0], "tensor")


def gain_of(norm_gain, x):
    return lax.dynamic_slice(norm_gain, (x * QUARTER,), (QUARTER,)).reshape(1, QUARTER)


def solution(mesh):
    split = Mesh(mesh.devices.reshape(8, 8, 2, 4), ALL)
    in_specs = (
        P(DP, "tensor"),
        P(ALL, None),
        P("tensor", DP),
        P(),
        P(DP, None, "tensor"),
        P(ALL, None),
        P(DP, None),
        P(),
        P(),
    )
    out_specs = (P(DP, "tensor"), P(DP))
    return jax.shard_map(body, mesh=split, in_specs=in_specs, out_specs=out_specs, check_vma=False)
```

```python
import jax
import jax.numpy as jnp
from jax import lax
from jax.experimental import pallas as pl
from jax.experimental.pallas import tpu as pltpu
from jax.sharding import Mesh, PartitionSpec as P

DP = ("z", "y", "core")
ALL = ("z", "y", "core", "tensor")
BF = jnp.bfloat16
F32 = jnp.float32
NT = (((1,), (1,)), ((), ()))
SMEM = pl.BlockSpec(memory_space=pltpu.SMEM)
VMEM = pl.BlockSpec(memory_space=pltpu.VMEM)
TOK, QUARTER, HALF = 512, 896, 448
DOCS, SLOTS, MEMBERS, SHARE = 128, 256, 512, 128


def params(mib=20):
    return pltpu.CompilerParams(vmem_limit_bytes=mib * 1024 * 1024)


def cost(flops, nbytes):
    return pl.CostEstimate(flops=flops, bytes_accessed=nbytes, transcendentals=0)


def device(z, y, core, x):
    return ((z * 8 + y) * 2 + core) * 4 + x


def placed(core, ring, line):
    return (ring, line) if core == 0 else (line, ring)


def grid():
    return [(z, y, c, x) for z in range(8) for y in range(8) for c in range(2) for x in range(4)]


def spread(flip):
    pairs = []
    for z, y, core, x in grid():
        to = core ^ flip
        to_z, to_y = placed(to, 2 * x + z % 2, y)
        pairs.append((device(z, y, core, x), device(to_z, to_y, to, z // 2)))
    return pairs


def groups(along):
    found = []
    for core in range(2):
        for x in range(4):
            for other in range(8):
                over_z = (along == "ring") == (core == 0)
                found.append(
                    [device(i, other, core, x) if over_z else device(other, i, core, x) for i in range(8)]
                )
    return found


def pair(value, turn):
    pairs = []
    for z, y, core, x in grid():
        pairs.append((device(z, y, core, x), device(z, y, core, x ^ (1 if core == turn else 3))))
    return lax.ppermute(value, ALL, pairs)


def core_swap(value):
    return lax.ppermute(value, ALL, [(at, at ^ 4) for at in range(512)])


def pack_kernel(place, context, residual, small, near, side):
    near[0:TOK, :] = context[...]
    side[0:TOK, :] = context[...]
    for out, row, target in ((near, 512, 1), (near, 640, 3), (side, 512, 2)):
        start = pl.multiple_of(place[target] * QUARTER, 128)
        out[row : row + 128, :] = residual[:, pl.ds(start, QUARTER)]
    near[768:784, :] = small[...]
    side[640:656, :] = small[...]


def project_kernel(
    place, context, near, side, far, weight, res, hidden, squares, ctx, tails, blocks, sems
):
    def fetch(source, target, at):
        return pltpu.make_async_copy(source, target, sems.at[at])

    copies = []
    for index, piece in enumerate((context, near, side, far)):
        start = pl.multiple_of(place[index] * QUARTER, QUARTER)
        copies.append(
            (
                fetch(piece.at[pl.ds(0, TOK), :], ctx.at[index], 2 * index),
                fetch(weight.at[pl.ds(start, QUARTER), :], blocks.at[index], 2 * index + 1),
            )
        )
    ends = [
        fetch(piece.at[pl.ds(row, 128), :], tails.at[index], 8 + index)
        for index, (piece, row) in enumerate(((res, 0), (near, 512), (side, 512), (far, 640)))
    ]
    for pair_of in copies:
        for copy in pair_of:
            copy.start()
    for copy in ends:
        copy.start()
    for index in range(4):
        for copy in copies[index]:
            copy.wait()
        product = lax.dot_general(ctx[index], blocks[index], NT, preferred_element_type=F32)
        if index == 0:
            hidden[...] = product
        else:
            hidden[...] += product
    for copy in ends:
        copy.wait()
    squares[...] = jnp.zeros_like(squares)
    for index in range(4):
        at = place[index]
        rows = pl.ds(pl.multiple_of(at * 128, 128), 128)
        value = hidden[rows, :] + tails[index].astype(F32)
        hidden[rows, :] = value
        sq = value * value
        part = sq[:, 0:128]
        for tile in range(1, 7):
            part = part + sq[:, tile * 128 : tile * 128 + 128]
        squares[pl.ds(at, 1), :] = jnp.sum(part.T, axis=0, keepdims=True)


def pool_kernel(hidden, gain, pool, inverse, total, slots, squares):
    scale = lax.rsqrt(total[...] / 3584.0 + 1e-06)
    summed = None
    for pack in range(4):
        rows = pl.ds(pack * 128, 128)
        column = jnp.broadcast_to(scale[pack : pack + 1, :], (128, 128)).T
        column = jnp.concatenate([column] * 7, axis=1)
        normed = (hidden[rows, :] * column * gain[...]).astype(BF)
        term = jnp.dot(pool[:, pack * 128 : pack * 128 + 128], normed, preferred_element_type=F32)
        summed = term if summed is None else summed + term
    pooled = summed * jnp.concatenate([inverse[...]] * 7, axis=1)
    slots[...] = pooled.astype(BF)
    sq = pooled * pooled
    part = sq[:, 0:128]
    for tile in range(1, 7):
        part = part + sq[:, tile * 128 : tile * 128 + 128]
    squares[...] = jnp.zeros_like(squares)
    for block in range(2):
        squares[pl.ds(block, 1), :] = jnp.sum(
            part[block * 128 : block * 128 + 128, :].T, axis=0, keepdims=True
        )


def dots_kernel(arrived, members, factor, out):
    for part in range(4):
        rows = pl.ds(part * SHARE, SHARE)
        dots = lax.dot_general(arrived[...], members[rows, :], NT, preferred_element_type=F32)
        out[:, part * SHARE : part * SHARE + SHARE] = (dots * factor[pl.ds(part, 1), :]).astype(BF)


def home_kernel(returned, pick, scale, live, scores, best):
    rows = jnp.dot(pick[...], returned[...], preferred_element_type=F32) * scale[...]
    scores[...] = rows
    masked = jnp.where(live[...] > 0.0, rows, -1000000000.0)
    best[...] = jnp.broadcast_to(jnp.max(masked.T, axis=0, keepdims=True), (8, 128))


def body(
    context,
    residual,
    out_weight,
    norm_gain,
    members,
    doc_lengths,
    doc_cluster,
    owner_map,
    member_counts,
):
    z, y = lax.axis_index("z"), lax.axis_index("y")
    core, x = lax.axis_index("core"), lax.axis_index("tensor")

    first = core == 0
    near_x = jnp.where(first, x ^ 1, x ^ 3)
    side_x = jnp.where(first, x ^ 3, x ^ 1)
    far_x = x ^ 2
    place = jnp.stack([x, near_x, side_x, far_x]).astype(jnp.int32)

    weight = out_weight.T
    keep = lax.ppermute(weight, ALL, spread(0))
    cross = lax.ppermute(weight, ALL, spread(1))
    block = jnp.concatenate(
        [jnp.where(first, keep, cross), jnp.where(first, cross, keep)], axis=0
    )

    resident = members[0]
    resident_f = resident.astype(F32)
    partial_sq = jnp.sum(resident_f * resident_f, axis=-1).astype(BF)
    small = jnp.concatenate(
        [partial_sq.reshape(4, 128), jnp.pad(doc_lengths.astype(BF), ((0, 0), (0, 96)))], axis=0
    )
    small = jnp.pad(small, ((0, 11), (0, QUARTER - 128)))
    to_near, to_side = pl.pallas_call(
        pack_kernel,
        out_shape=(
            jax.ShapeDtypeStruct((784, QUARTER), BF),
            jax.ShapeDtypeStruct((656, QUARTER), BF),
        ),
        in_specs=[SMEM] + [VMEM] * 3,
        out_specs=(pl.BlockSpec(), pl.BlockSpec()),
        compiler_params=params(),
        cost_estimate=cost(0, 6_000_000),
        name="pack",
    )(place, context, residual, small)

    near = pair(to_near, 0)
    plane = lax.all_to_all(
        jnp.broadcast_to(block[None], (8, 56, QUARTER)), ALL, 0, 0,
        axis_index_groups=groups("line"), tiled=True,
    ).reshape(HALF, QUARTER)
    plane, _, _ = lax.optimization_barrier((plane, to_near, to_side))
    plane = lax.all_gather(plane, ALL, axis=0, axis_index_groups=groups("ring"), tiled=True)
    near, late_side = lax.optimization_barrier((near, to_side))
    far, side = pair(near, 1), pair(late_side, 1)

    tails = [(x, small), (near_x, near[-16:]), (side_x, side[-16:]), (far_x, far[-16:])]
    member_sq = sum((tail[:4, :128].astype(F32) for _, tail in tails[1:]), small[:4, :128].astype(F32))
    lens = jnp.zeros((4, 32), F32)
    for at, tail in tails:
        lens = lax.dynamic_update_slice(lens, tail[4:5, :32].astype(F32), (at, 0))

    cluster_ids = jnp.arange(owner_map.shape[0], dtype=jnp.int32)
    matches = doc_cluster[:, 0][:, None] == cluster_ids[None, :]
    doc_owner = jnp.sum(jnp.where(matches, owner_map[None, :], 0), axis=1)
    doc_members = jnp.sum(jnp.where(matches, member_counts[None, :], 0), axis=1)
    doc_order = jnp.arange(DOCS, dtype=jnp.int32)
    same_owner = (doc_owner[:, None] == doc_owner[None, :]) & (
        doc_order[:, None] > doc_order[None, :]
    )
    doc_slot = doc_owner * 2 + jnp.sum(same_owner.astype(jnp.int32), axis=1)
    slot_ids = jnp.arange(SLOTS, dtype=jnp.int32)
    select = slot_ids[:, None] == doc_slot[None, :]
    wide_ids = jnp.arange(4 * SLOTS, dtype=jnp.int32)
    wide_ids = lax.div(wide_ids, 8) * 2 + lax.rem(wide_ids, 2)
    pick = (doc_slot[:, None] == wide_ids[None, :]).astype(BF)
    lens_int = lens.astype(jnp.int32)
    ends = jnp.cumsum(lens_int, axis=1)
    offsets = 128 * jnp.arange(4, dtype=jnp.int32)[:, None]
    doc_begin = (ends - lens_int + offsets).reshape(DOCS)
    doc_end = (ends + offsets).reshape(DOCS)
    tokens = jnp.arange(TOK, dtype=jnp.int32)
    inside = (tokens[None, :] >= doc_begin[:, None]) & (tokens[None, :] < doc_end[:, None])
    pool = jnp.dot(select.astype(BF), inside.astype(BF), preferred_element_type=F32).astype(BF)
    slot_len = jnp.sum(jnp.where(select, lens.reshape(DOCS)[None, :], 0.0), axis=1)
    inverse = jnp.broadcast_to((1.0 / jnp.maximum(slot_len, 1.0))[:, None], (SLOTS, 128))
    columns = x * SHARE + jnp.arange(SHARE, dtype=jnp.int32)
    live = (columns[None, :] < doc_members[:, None]).astype(F32)

    own_dp = (z * 8 + y) * 2 + core
    own_count = jnp.sum(jnp.where(owner_map == own_dp, member_counts, 0))
    member_ids = jnp.arange(MEMBERS, dtype=jnp.int32).reshape(4, 128)
    factor = jnp.where(member_ids < own_count, lax.rsqrt(member_sq / 3584.0 + 1e-06), 0.0)

    res = lax.dynamic_slice(residual, (0, x * QUARTER), (128, QUARTER))
    hidden, squares = pl.pallas_call(
        project_kernel,
        out_shape=(
            jax.ShapeDtypeStruct((TOK, QUARTER), F32),
            jax.ShapeDtypeStruct((8, 128), F32),
        ),
        in_specs=[SMEM] + [pl.BlockSpec(memory_space=pl.ANY)] * 6,
        out_specs=(VMEM, VMEM),
        scratch_shapes=[
            pltpu.VMEM((4, TOK, QUARTER), BF),
            pltpu.VMEM((4, 128, QUARTER), BF),
            pltpu.VMEM((4, QUARTER, QUARTER), BF),
            pltpu.SemaphoreType.DMA((12,)),
        ],
        compiler_params=params(54),
        cost_estimate=cost(2 * TOK * QUARTER * 3584, 13_000_000),
        name="project",
    )(place, context, near, side, far, plane, res)

    slots, doc_sq = pl.pallas_call(
        pool_kernel,
        out_shape=(
            jax.ShapeDtypeStruct((SLOTS, QUARTER), BF),
            jax.ShapeDtypeStruct((8, 128), F32),
        ),
        in_specs=[VMEM] * 5,
        out_specs=(VMEM, VMEM),
        compiler_params=params(),
        cost_estimate=cost(2 * SLOTS * TOK * QUARTER, 3_000_000),
        name="pool",
    )(hidden, gain_of(norm_gain, x), pool, inverse, lax.psum(squares, "tensor"))

    arrived = lax.all_to_all(
        slots.reshape(DOCS, 2, QUARTER), DP, split_axis=0, concat_axis=0, tiled=True
    ).reshape(SLOTS, QUARTER)

    slot_sq = lax.psum(doc_sq, "tensor")[:2].reshape(SLOTS)
    doc_total = jnp.sum(jnp.where(select, slot_sq[:, None], 0.0), axis=0)
    scale = jnp.broadcast_to(lax.rsqrt(doc_total + 1e-06)[:, None], (DOCS, SHARE))

    partial = pl.pallas_call(
        dots_kernel,
        out_shape=jax.ShapeDtypeStruct((SLOTS, MEMBERS), BF),
        in_specs=[VMEM] * 3,
        out_specs=VMEM,
        compiler_params=params(),
        cost_estimate=cost(2 * SLOTS * MEMBERS * QUARTER, 2_000_000),
        name="dots",
    )(arrived, resident, factor)

    partial = partial.reshape(DOCS, 2, 4, SHARE).transpose(0, 2, 1, 3).reshape(4 * DOCS, 2, SHARE)
    returned = lax.all_to_all(partial, ALL, split_axis=0, concat_axis=0, tiled=True)
    returned = returned.reshape(4 * SLOTS, SHARE)
    scores, best = pl.pallas_call(
        home_kernel,
        out_shape=(
            jax.ShapeDtypeStruct((DOCS, SHARE), F32),
            jax.ShapeDtypeStruct((8, 128), F32),
        ),
        in_specs=[VMEM] * 4,
        out_specs=(VMEM, VMEM),
        compiler_params=params(),
        cost_estimate=cost(2 * SLOTS * DOCS * SHARE, 400_000),
        name="home",
    )(returned, pick, scale, live)
    return scores, lax.pmax(best[0], "tensor")


def gain_of(norm_gain, x):
    return lax.dynamic_slice(norm_gain, (x * QUARTER,), (QUARTER,)).reshape(1, QUARTER)


def solution(mesh):
    split = Mesh(mesh.devices.reshape(8, 8, 2, 4), ALL)
    in_specs = (
        P(DP, "tensor"),
        P(ALL, None),
        P("tensor", DP),
        P(),
        P(DP, None, "tensor"),
        P(ALL, None),
        P(DP, None),
        P(),
        P(),
    )
    out_specs = (P(DP, "tensor"), P(DP))
    return jax.shard_map(body, mesh=split, in_specs=in_specs, out_specs=out_specs, check_vma=False)
```

```python
import jax
import jax.numpy as jnp
from jax import lax
from jax.experimental import pallas as pl
from jax.experimental.pallas import tpu as pltpu
from jax.sharding import Mesh, PartitionSpec as P

DP = ("z", "y", "core")
ALL = ("z", "y", "core", "tensor")
BF = jnp.bfloat16
F32 = jnp.float32
NT = (((1,), (1,)), ((), ()))
SMEM = pl.BlockSpec(memory_space=pltpu.SMEM)
VMEM = pl.BlockSpec(memory_space=pltpu.VMEM)
TOK, QUARTER, HALF = 512, 896, 448
DOCS, SLOTS, MEMBERS, SHARE = 128, 256, 512, 128


def params(mib=20):
    return pltpu.CompilerParams(vmem_limit_bytes=mib * 1024 * 1024)


def cost(flops, nbytes):
    return pl.CostEstimate(flops=flops, bytes_accessed=nbytes, transcendentals=0)


def device(z, y, core, x):
    return ((z * 8 + y) * 2 + core) * 4 + x


def placed(core, ring, line):
    return (ring, line) if core == 0 else (line, ring)


def grid():
    return [(z, y, c, x) for z in range(8) for y in range(8) for c in range(2) for x in range(4)]


def spread(flip):
    pairs = []
    for z, y, core, x in grid():
        to = core ^ flip
        to_z, to_y = placed(to, 2 * x + z % 2, y)
        pairs.append((device(z, y, core, x), device(to_z, to_y, to, z // 2)))
    return pairs


def groups(along):
    found = []
    for core in range(2):
        for x in range(4):
            for other in range(8):
                over_z = (along == "ring") == (core == 0)
                found.append(
                    [device(i, other, core, x) if over_z else device(other, i, core, x) for i in range(8)]
                )
    return found


def pair(value, turn):
    pairs = []
    for z, y, core, x in grid():
        pairs.append((device(z, y, core, x), device(z, y, core, x ^ (1 if core == turn else 3))))
    return lax.ppermute(value, ALL, pairs)


def core_swap(value):
    return lax.ppermute(value, ALL, [(at, at ^ 4) for at in range(512)])


def pack_kernel(place, context, residual, small, near, rest, side):
    for out, row, target in ((near, 0, 1), (near, 128, 3), (side, 512, 2)):
        start = pl.multiple_of(place[target] * QUARTER, 128)
        out[row : row + 128, :] = residual[:, pl.ds(start, QUARTER)]
    near[256:272, :] = small[...]
    near[272:400, :] = context[0:128, :]
    rest[...] = context[128:TOK, :]
    side[0:TOK, :] = context[...]
    side[640:656, :] = small[...]


def project_kernel(
    place, context, near, near_rest, side, far, far_rest, weight, res, hidden, squares,
    ctx, tails, blocks, sems,
):
    def fetch(source, target, at):
        return pltpu.make_async_copy(source, target, sems.at[at])

    pieces = (
        ((context, 0, 0, TOK),),
        ((near, 272, 0, 128), (near_rest, 0, 128, 384)),
        ((side, 0, 0, TOK),),
        ((far, 272, 0, 128), (far_rest, 0, 128, 384)),
    )
    copies, used = [], 0
    for index, parts in enumerate(pieces):
        start = pl.multiple_of(place[index] * QUARTER, QUARTER)
        group = [fetch(weight.at[pl.ds(start, QUARTER), :], blocks.at[index], used)]
        used += 1
        for piece, row, to, count in parts:
            group.append(
                fetch(piece.at[pl.ds(row, count), :], ctx.at[index, pl.ds(to, count), :], used)
            )
            used += 1
        copies.append(group)
    ends = [
        fetch(piece.at[pl.ds(row, 128), :], tails.at[index], used + index)
        for index, (piece, row) in enumerate(((res, 0), (near, 0), (side, 512), (far, 128)))
    ]
    for pair_of in copies:
        for copy in pair_of:
            copy.start()
    for copy in ends:
        copy.start()
    for index in range(4):
        for copy in copies[index]:
            copy.wait()
        product = lax.dot_general(ctx[index], blocks[index], NT, preferred_element_type=F32)
        if index == 0:
            hidden[...] = product
        else:
            hidden[...] += product
    for copy in ends:
        copy.wait()
    squares[...] = jnp.zeros_like(squares)
    for index in range(4):
        at = place[index]
        rows = pl.ds(pl.multiple_of(at * 128, 128), 128)
        value = hidden[rows, :] + tails[index].astype(F32)
        hidden[rows, :] = value
        sq = value * value
        part = sq[:, 0:128]
        for tile in range(1, 7):
            part = part + sq[:, tile * 128 : tile * 128 + 128]
        squares[pl.ds(at, 1), :] = jnp.sum(part.T, axis=0, keepdims=True)


def pool_kernel(hidden, gain, pool, inverse, total, slots, squares):
    scale = lax.rsqrt(total[...] / 3584.0 + 1e-06)
    summed = None
    for pack in range(4):
        rows = pl.ds(pack * 128, 128)
        column = jnp.broadcast_to(scale[pack : pack + 1, :], (128, 128)).T
        column = jnp.concatenate([column] * 7, axis=1)
        normed = (hidden[rows, :] * column * gain[...]).astype(BF)
        term = jnp.dot(pool[:, pack * 128 : pack * 128 + 128], normed, preferred_element_type=F32)
        summed = term if summed is None else summed + term
    pooled = summed * jnp.concatenate([inverse[...]] * 7, axis=1)
    slots[...] = pooled.astype(BF)
    sq = pooled * pooled
    part = sq[:, 0:128]
    for tile in range(1, 7):
        part = part + sq[:, tile * 128 : tile * 128 + 128]
    squares[...] = jnp.zeros_like(squares)
    for block in range(2):
        squares[pl.ds(block, 1), :] = jnp.sum(
            part[block * 128 : block * 128 + 128, :].T, axis=0, keepdims=True
        )


def dots_kernel(arrived, members, factor, out):
    for part in range(4):
        rows = pl.ds(part * SHARE, SHARE)
        dots = lax.dot_general(arrived[...], members[rows, :], NT, preferred_element_type=F32)
        out[:, part * SHARE : part * SHARE + SHARE] = (dots * factor[pl.ds(part, 1), :]).astype(BF)


def home_kernel(returned, pick, scale, live, scores, best):
    rows = jnp.dot(pick[...], returned[...], preferred_element_type=F32) * scale[...]
    scores[...] = rows
    masked = jnp.where(live[...] > 0.0, rows, -1000000000.0)
    best[...] = jnp.broadcast_to(jnp.max(masked.T, axis=0, keepdims=True), (8, 128))


def body(
    context,
    residual,
    out_weight,
    norm_gain,
    members,
    doc_lengths,
    doc_cluster,
    owner_map,
    member_counts,
):
    z, y = lax.axis_index("z"), lax.axis_index("y")
    core, x = lax.axis_index("core"), lax.axis_index("tensor")

    first = core == 0
    near_x = jnp.where(first, x ^ 1, x ^ 3)
    side_x = jnp.where(first, x ^ 3, x ^ 1)
    far_x = x ^ 2
    place = jnp.stack([x, near_x, side_x, far_x]).astype(jnp.int32)

    weight = out_weight.T
    keep = lax.ppermute(weight, ALL, spread(0))
    cross = lax.ppermute(weight, ALL, spread(1))
    block = jnp.concatenate(
        [jnp.where(first, keep, cross), jnp.where(first, cross, keep)], axis=0
    )

    resident = members[0]
    resident_f = resident.astype(F32)
    partial_sq = jnp.sum(resident_f * resident_f, axis=-1).astype(BF)
    small = jnp.concatenate(
        [partial_sq.reshape(4, 128), jnp.pad(doc_lengths.astype(BF), ((0, 0), (0, 96)))], axis=0
    )
    small = jnp.pad(small, ((0, 11), (0, QUARTER - 128)))
    to_near, to_rest, to_side = pl.pallas_call(
        pack_kernel,
        out_shape=(
            jax.ShapeDtypeStruct((400, QUARTER), BF),
            jax.ShapeDtypeStruct((384, QUARTER), BF),
            jax.ShapeDtypeStruct((656, QUARTER), BF),
        ),
        in_specs=[SMEM] + [VMEM] * 3,
        out_specs=(pl.BlockSpec(),) * 3,
        compiler_params=params(),
        cost_estimate=cost(0, 6_000_000),
        name="pack",
    )(place, context, residual, small)

    near = pair(to_near, 0)
    plane = lax.all_to_all(
        jnp.broadcast_to(block[None], (8, 56, QUARTER)), ALL, 0, 0,
        axis_index_groups=groups("line"), tiled=True,
    ).reshape(HALF, QUARTER)
    plane, near, _, _ = lax.optimization_barrier((plane, near, to_rest, to_side))
    plane = lax.all_gather(plane, ALL, axis=0, axis_index_groups=groups("ring"), tiled=True)
    near_rest, far = pair(to_rest, 0), pair(near, 1)
    near_rest, late_side = lax.optimization_barrier((near_rest, to_side))
    far_rest, side = pair(near_rest, 1), pair(late_side, 1)

    tails = [(x, small), (near_x, near[256:272]), (side_x, side[-16:]), (far_x, far[256:272])]
    member_sq = sum((tail[:4, :128].astype(F32) for _, tail in tails[1:]), small[:4, :128].astype(F32))
    lens = jnp.zeros((4, 32), F32)
    for at, tail in tails:
        lens = lax.dynamic_update_slice(lens, tail[4:5, :32].astype(F32), (at, 0))

    cluster_ids = jnp.arange(owner_map.shape[0], dtype=jnp.int32)
    matches = doc_cluster[:, 0][:, None] == cluster_ids[None, :]
    doc_owner = jnp.sum(jnp.where(matches, owner_map[None, :], 0), axis=1)
    doc_members = jnp.sum(jnp.where(matches, member_counts[None, :], 0), axis=1)
    doc_order = jnp.arange(DOCS, dtype=jnp.int32)
    same_owner = (doc_owner[:, None] == doc_owner[None, :]) & (
        doc_order[:, None] > doc_order[None, :]
    )
    doc_slot = doc_owner * 2 + jnp.sum(same_owner.astype(jnp.int32), axis=1)
    slot_ids = jnp.arange(SLOTS, dtype=jnp.int32)
    select = slot_ids[:, None] == doc_slot[None, :]
    wide_ids = jnp.arange(4 * SLOTS, dtype=jnp.int32)
    wide_ids = lax.div(wide_ids, 8) * 2 + lax.rem(wide_ids, 2)
    pick = (doc_slot[:, None] == wide_ids[None, :]).astype(BF)
    lens_int = lens.astype(jnp.int32)
    ends = jnp.cumsum(lens_int, axis=1)
    offsets = 128 * jnp.arange(4, dtype=jnp.int32)[:, None]
    doc_begin = (ends - lens_int + offsets).reshape(DOCS)
    doc_end = (ends + offsets).reshape(DOCS)
    tokens = jnp.arange(TOK, dtype=jnp.int32)
    inside = (tokens[None, :] >= doc_begin[:, None]) & (tokens[None, :] < doc_end[:, None])
    pool = jnp.dot(select.astype(BF), inside.astype(BF), preferred_element_type=F32).astype(BF)
    slot_len = jnp.sum(jnp.where(select, lens.reshape(DOCS)[None, :], 0.0), axis=1)
    inverse = jnp.broadcast_to((1.0 / jnp.maximum(slot_len, 1.0))[:, None], (SLOTS, 128))
    columns = x * SHARE + jnp.arange(SHARE, dtype=jnp.int32)
    live = (columns[None, :] < doc_members[:, None]).astype(F32)

    own_dp = (z * 8 + y) * 2 + core
    own_count = jnp.sum(jnp.where(owner_map == own_dp, member_counts, 0))
    member_ids = jnp.arange(MEMBERS, dtype=jnp.int32).reshape(4, 128)
    factor = jnp.where(member_ids < own_count, lax.rsqrt(member_sq / 3584.0 + 1e-06), 0.0)

    res = lax.dynamic_slice(residual, (0, x * QUARTER), (128, QUARTER))
    hidden, squares = pl.pallas_call(
        project_kernel,
        out_shape=(
            jax.ShapeDtypeStruct((TOK, QUARTER), F32),
            jax.ShapeDtypeStruct((8, 128), F32),
        ),
        in_specs=[SMEM] + [pl.BlockSpec(memory_space=pl.ANY)] * 8,
        out_specs=(VMEM, VMEM),
        scratch_shapes=[
            pltpu.VMEM((4, TOK, QUARTER), BF),
            pltpu.VMEM((4, 128, QUARTER), BF),
            pltpu.VMEM((4, QUARTER, QUARTER), BF),
            pltpu.SemaphoreType.DMA((14,)),
        ],
        compiler_params=params(54),
        cost_estimate=cost(2 * TOK * QUARTER * 3584, 13_000_000),
        name="project",
    )(place, context, near, near_rest, side, far, far_rest, plane, res)

    slots, doc_sq = pl.pallas_call(
        pool_kernel,
        out_shape=(
            jax.ShapeDtypeStruct((SLOTS, QUARTER), BF),
            jax.ShapeDtypeStruct((8, 128), F32),
        ),
        in_specs=[VMEM] * 5,
        out_specs=(VMEM, VMEM),
        compiler_params=params(),
        cost_estimate=cost(2 * SLOTS * TOK * QUARTER, 3_000_000),
        name="pool",
    )(hidden, gain_of(norm_gain, x), pool, inverse, lax.psum(squares, "tensor"))

    arrived = lax.all_to_all(
        slots.reshape(DOCS, 2, QUARTER), DP, split_axis=0, concat_axis=0, tiled=True
    ).reshape(SLOTS, QUARTER)

    slot_sq = lax.psum(doc_sq, "tensor")[:2].reshape(SLOTS)
    doc_total = jnp.sum(jnp.where(select, slot_sq[:, None], 0.0), axis=0)
    scale = jnp.broadcast_to(lax.rsqrt(doc_total + 1e-06)[:, None], (DOCS, SHARE))

    partial = pl.pallas_call(
        dots_kernel,
        out_shape=jax.ShapeDtypeStruct((SLOTS, MEMBERS), BF),
        in_specs=[VMEM] * 3,
        out_specs=VMEM,
        compiler_params=params(),
        cost_estimate=cost(2 * SLOTS * MEMBERS * QUARTER, 2_000_000),
        name="dots",
    )(arrived, resident, factor)

    partial = partial.reshape(DOCS, 2, 4, SHARE).transpose(0, 2, 1, 3).reshape(4 * DOCS, 2, SHARE)
    returned = lax.all_to_all(partial, ALL, split_axis=0, concat_axis=0, tiled=True)
    returned = returned.reshape(4 * SLOTS, SHARE)
    scores, best = pl.pallas_call(
        home_kernel,
        out_shape=(
            jax.ShapeDtypeStruct((DOCS, SHARE), F32),
            jax.ShapeDtypeStruct((8, 128), F32),
        ),
        in_specs=[VMEM] * 4,
        out_specs=(VMEM, VMEM),
        compiler_params=params(),
        cost_estimate=cost(2 * SLOTS * DOCS * SHARE, 400_000),
        name="home",
    )(returned, pick, scale, live)
    return scores, lax.pmax(best[0], "tensor")


def gain_of(norm_gain, x):
    return lax.dynamic_slice(norm_gain, (x * QUARTER,), (QUARTER,)).reshape(1, QUARTER)


def solution(mesh):
    split = Mesh(mesh.devices.reshape(8, 8, 2, 4), ALL)
    in_specs = (
        P(DP, "tensor"),
        P(ALL, None),
        P("tensor", DP),
        P(),
        P(DP, None, "tensor"),
        P(ALL, None),
        P(DP, None),
        P(),
        P(),
    )
    out_specs = (P(DP, "tensor"), P(DP))
    return jax.shard_map(body, mesh=split, in_specs=in_specs, out_specs=out_specs, check_vma=False)
```

```python
import jax
import jax.numpy as jnp
from jax import lax
from jax.experimental import pallas as pl
from jax.experimental.pallas import tpu as pltpu
from jax.sharding import Mesh, PartitionSpec as P

DP = ("z", "y", "core")
ALL = ("z", "y", "core", "tensor")
BF = jnp.bfloat16
F32 = jnp.float32
NT = (((1,), (1,)), ((), ()))
SMEM = pl.BlockSpec(memory_space=pltpu.SMEM)
VMEM = pl.BlockSpec(memory_space=pltpu.VMEM)
TOK, QUARTER, HALF = 512, 896, 448
DOCS, SLOTS, MEMBERS, SHARE = 128, 256, 512, 128


def params(mib=20):
    return pltpu.CompilerParams(vmem_limit_bytes=mib * 1024 * 1024)


def cost(flops, nbytes):
    return pl.CostEstimate(flops=flops, bytes_accessed=nbytes, transcendentals=0)


def device(z, y, core, x):
    return ((z * 8 + y) * 2 + core) * 4 + x


def placed(core, ring, line):
    return (ring, line) if core == 0 else (line, ring)


def grid():
    return [(z, y, c, x) for z in range(8) for y in range(8) for c in range(2) for x in range(4)]


def spread():
    pairs = []
    for z, y, core, x in grid():
        to_z, to_y = placed(core, 2 * x + z % 2, y)
        pairs.append((device(z, y, core, x), device(to_z, to_y, core, z // 2)))
    return pairs


def groups(along):
    found = []
    for core in range(2):
        for x in range(4):
            for other in range(8):
                over_z = (along == "ring") == (core == 0)
                found.append(
                    [device(i, other, core, x) if over_z else device(other, i, core, x) for i in range(8)]
                )
    return found


def pair(value, turn):
    pairs = []
    for z, y, core, x in grid():
        pairs.append((device(z, y, core, x), device(z, y, core, x ^ (1 if core == turn else 3))))
    return lax.ppermute(value, ALL, pairs)


def core_swap(value):
    return lax.ppermute(value, ALL, [(at, at ^ 4) for at in range(512)])


def pack_kernel(place, context, residual, small, near, rest, side):
    for out, row, target in ((near, 0, 1), (near, 128, 3), (side, 512, 2)):
        start = pl.multiple_of(place[target] * QUARTER, 128)
        out[row : row + 128, :] = residual[:, pl.ds(start, QUARTER)]
    near[256:272, :] = small[...]
    near[272:400, :] = context[0:128, :]
    rest[...] = context[128:TOK, :]
    side[0:TOK, :] = context[...]
    side[640:656, :] = small[...]


def project_kernel(
    place, context, near, near_rest, side, far, far_rest, weight, res, hidden, squares,
    ctx, tails, blocks, sems,
):
    def fetch(source, target, at):
        return pltpu.make_async_copy(source, target, sems.at[at])

    pieces = (
        ((context, 0, 0, TOK),),
        ((near, 272, 0, 128), (near_rest, 0, 128, 384)),
        ((side, 0, 0, TOK),),
        ((far, 272, 0, 128), (far_rest, 0, 128, 384)),
    )
    copies, used = [], 0
    for index, parts in enumerate(pieces):
        start = pl.multiple_of(place[index] * QUARTER, QUARTER)
        group = [fetch(weight.at[pl.ds(start, QUARTER), :], blocks.at[index], used)]
        used += 1
        for piece, row, to, count in parts:
            group.append(
                fetch(piece.at[pl.ds(row, count), :], ctx.at[index, pl.ds(to, count), :], used)
            )
            used += 1
        copies.append(group)
    ends = [
        fetch(piece.at[pl.ds(row, 128), :], tails.at[index], used + index)
        for index, (piece, row) in enumerate(((res, 0), (near, 0), (side, 512), (far, 128)))
    ]
    for pair_of in copies:
        for copy in pair_of:
            copy.start()
    for copy in ends:
        copy.start()
    for index in range(4):
        for copy in copies[index]:
            copy.wait()
        product = lax.dot_general(ctx[index], blocks[index], NT, preferred_element_type=F32)
        if index == 0:
            hidden[...] = product
        else:
            hidden[...] += product
    for copy in ends:
        copy.wait()
    squares[...] = jnp.zeros_like(squares)
    for index in range(4):
        at = place[index]
        rows = pl.ds(pl.multiple_of(at * 128, 128), 128)
        value = hidden[rows, :] + tails[index].astype(F32)
        hidden[rows, :] = value
        sq = value * value
        part = sq[:, 0:128]
        for tile in range(1, 7):
            part = part + sq[:, tile * 128 : tile * 128 + 128]
        squares[pl.ds(at, 1), :] = jnp.sum(part.T, axis=0, keepdims=True)


def pool_kernel(hidden, gain, pool, inverse, total, slots, squares):
    scale = lax.rsqrt(total[...] / 3584.0 + 1e-06)
    summed = None
    for pack in range(4):
        rows = pl.ds(pack * 128, 128)
        column = jnp.broadcast_to(scale[pack : pack + 1, :], (128, 128)).T
        column = jnp.concatenate([column] * 7, axis=1)
        normed = (hidden[rows, :] * column * gain[...]).astype(BF)
        term = jnp.dot(pool[:, pack * 128 : pack * 128 + 128], normed, preferred_element_type=F32)
        summed = term if summed is None else summed + term
    pooled = summed * jnp.concatenate([inverse[...]] * 7, axis=1)
    slots[...] = pooled.astype(BF)
    sq = pooled * pooled
    part = sq[:, 0:128]
    for tile in range(1, 7):
        part = part + sq[:, tile * 128 : tile * 128 + 128]
    squares[...] = jnp.zeros_like(squares)
    for block in range(2):
        squares[pl.ds(block, 1), :] = jnp.sum(
            part[block * 128 : block * 128 + 128, :].T, axis=0, keepdims=True
        )


def dots_kernel(arrived, members, factor, out):
    for part in range(4):
        rows = pl.ds(part * SHARE, SHARE)
        dots = lax.dot_general(arrived[...], members[rows, :], NT, preferred_element_type=F32)
        out[:, part * SHARE : part * SHARE + SHARE] = (dots * factor[pl.ds(part, 1), :]).astype(BF)


def home_kernel(returned, pick, scale, live, scores, best):
    rows = jnp.dot(pick[...], returned[...], preferred_element_type=F32) * scale[...]
    scores[...] = rows
    masked = jnp.where(live[...] > 0.0, rows, -1000000000.0)
    best[...] = jnp.broadcast_to(jnp.max(masked.T, axis=0, keepdims=True), (8, 128))


def body(
    context,
    residual,
    out_weight,
    norm_gain,
    members,
    doc_lengths,
    doc_cluster,
    owner_map,
    member_counts,
):
    z, y = lax.axis_index("z"), lax.axis_index("y")
    core, x = lax.axis_index("core"), lax.axis_index("tensor")

    first = core == 0
    near_x = jnp.where(first, x ^ 1, x ^ 3)
    side_x = jnp.where(first, x ^ 3, x ^ 1)
    far_x = x ^ 2
    place = jnp.stack([x, near_x, side_x, far_x]).astype(jnp.int32)

    weight = out_weight.T
    twin = core_swap(weight)
    block = jnp.concatenate(
        [jnp.where(first, weight, twin), jnp.where(first, twin, weight)], axis=0
    )
    block = lax.ppermute(block, ALL, spread())

    resident = members[0]
    resident_f = resident.astype(F32)
    partial_sq = jnp.sum(resident_f * resident_f, axis=-1).astype(BF)
    small = jnp.concatenate(
        [partial_sq.reshape(4, 128), jnp.pad(doc_lengths.astype(BF), ((0, 0), (0, 96)))], axis=0
    )
    small = jnp.pad(small, ((0, 11), (0, QUARTER - 128)))
    to_near, to_rest, to_side = pl.pallas_call(
        pack_kernel,
        out_shape=(
            jax.ShapeDtypeStruct((400, QUARTER), BF),
            jax.ShapeDtypeStruct((384, QUARTER), BF),
            jax.ShapeDtypeStruct((656, QUARTER), BF),
        ),
        in_specs=[SMEM] + [VMEM] * 3,
        out_specs=(pl.BlockSpec(),) * 3,
        compiler_params=params(),
        cost_estimate=cost(0, 6_000_000),
        name="pack",
    )(place, context, residual, small)

    near = pair(to_near, 0)
    plane = lax.all_to_all(
        jnp.broadcast_to(block[None], (8, 56, QUARTER)), ALL, 0, 0,
        axis_index_groups=groups("line"), tiled=True,
    ).reshape(HALF, QUARTER)
    plane, near, _, _ = lax.optimization_barrier((plane, near, to_rest, to_side))
    plane = lax.all_gather(plane, ALL, axis=0, axis_index_groups=groups("ring"), tiled=True)
    near_rest, far = pair(to_rest, 0), pair(near, 1)
    near_rest, late_side = lax.optimization_barrier((near_rest, to_side))
    far_rest, side = pair(near_rest, 1), pair(late_side, 1)

    tails = [(x, small), (near_x, near[256:272]), (side_x, side[-16:]), (far_x, far[256:272])]
    member_sq = sum((tail[:4, :128].astype(F32) for _, tail in tails[1:]), small[:4, :128].astype(F32))
    lens = jnp.zeros((4, 32), F32)
    for at, tail in tails:
        lens = lax.dynamic_update_slice(lens, tail[4:5, :32].astype(F32), (at, 0))

    cluster_ids = jnp.arange(owner_map.shape[0], dtype=jnp.int32)
    matches = doc_cluster[:, 0][:, None] == cluster_ids[None, :]
    doc_owner = jnp.sum(jnp.where(matches, owner_map[None, :], 0), axis=1)
    doc_members = jnp.sum(jnp.where(matches, member_counts[None, :], 0), axis=1)
    doc_order = jnp.arange(DOCS, dtype=jnp.int32)
    same_owner = (doc_owner[:, None] == doc_owner[None, :]) & (
        doc_order[:, None] > doc_order[None, :]
    )
    doc_slot = doc_owner * 2 + jnp.sum(same_owner.astype(jnp.int32), axis=1)
    slot_ids = jnp.arange(SLOTS, dtype=jnp.int32)
    select = slot_ids[:, None] == doc_slot[None, :]
    wide_ids = jnp.arange(4 * SLOTS, dtype=jnp.int32)
    wide_ids = lax.div(wide_ids, 8) * 2 + lax.rem(wide_ids, 2)
    pick = (doc_slot[:, None] == wide_ids[None, :]).astype(BF)
    lens_int = lens.astype(jnp.int32)
    ends = jnp.cumsum(lens_int, axis=1)
    offsets = 128 * jnp.arange(4, dtype=jnp.int32)[:, None]
    doc_begin = (ends - lens_int + offsets).reshape(DOCS)
    doc_end = (ends + offsets).reshape(DOCS)
    tokens = jnp.arange(TOK, dtype=jnp.int32)
    inside = (tokens[None, :] >= doc_begin[:, None]) & (tokens[None, :] < doc_end[:, None])
    pool = jnp.dot(select.astype(BF), inside.astype(BF), preferred_element_type=F32).astype(BF)
    slot_len = jnp.sum(jnp.where(select, lens.reshape(DOCS)[None, :], 0.0), axis=1)
    inverse = jnp.broadcast_to((1.0 / jnp.maximum(slot_len, 1.0))[:, None], (SLOTS, 128))
    columns = x * SHARE + jnp.arange(SHARE, dtype=jnp.int32)
    live = (columns[None, :] < doc_members[:, None]).astype(F32)

    own_dp = (z * 8 + y) * 2 + core
    own_count = jnp.sum(jnp.where(owner_map == own_dp, member_counts, 0))
    member_ids = jnp.arange(MEMBERS, dtype=jnp.int32).reshape(4, 128)
    factor = jnp.where(member_ids < own_count, lax.rsqrt(member_sq / 3584.0 + 1e-06), 0.0)

    res = lax.dynamic_slice(residual, (0, x * QUARTER), (128, QUARTER))
    hidden, squares = pl.pallas_call(
        project_kernel,
        out_shape=(
            jax.ShapeDtypeStruct((TOK, QUARTER), F32),
            jax.ShapeDtypeStruct((8, 128), F32),
        ),
        in_specs=[SMEM] + [pl.BlockSpec(memory_space=pl.ANY)] * 8,
        out_specs=(VMEM, VMEM),
        scratch_shapes=[
            pltpu.VMEM((4, TOK, QUARTER), BF),
            pltpu.VMEM((4, 128, QUARTER), BF),
            pltpu.VMEM((4, QUARTER, QUARTER), BF),
            pltpu.SemaphoreType.DMA((14,)),
        ],
        compiler_params=params(54),
        cost_estimate=cost(2 * TOK * QUARTER * 3584, 13_000_000),
        name="project",
    )(place, context, near, near_rest, side, far, far_rest, plane, res)

    slots, doc_sq = pl.pallas_call(
        pool_kernel,
        out_shape=(
            jax.ShapeDtypeStruct((SLOTS, QUARTER), BF),
            jax.ShapeDtypeStruct((8, 128), F32),
        ),
        in_specs=[VMEM] * 5,
        out_specs=(VMEM, VMEM),
        compiler_params=params(),
        cost_estimate=cost(2 * SLOTS * TOK * QUARTER, 3_000_000),
        name="pool",
    )(hidden, gain_of(norm_gain, x), pool, inverse, lax.psum(squares, "tensor"))

    arrived = lax.all_to_all(
        slots.reshape(DOCS, 2, QUARTER), DP, split_axis=0, concat_axis=0, tiled=True
    ).reshape(SLOTS, QUARTER)

    slot_sq = lax.psum(doc_sq, "tensor")[:2].reshape(SLOTS)
    doc_total = jnp.sum(jnp.where(select, slot_sq[:, None], 0.0), axis=0)
    scale = jnp.broadcast_to(lax.rsqrt(doc_total + 1e-06)[:, None], (DOCS, SHARE))

    partial = pl.pallas_call(
        dots_kernel,
        out_shape=jax.ShapeDtypeStruct((SLOTS, MEMBERS), BF),
        in_specs=[VMEM] * 3,
        out_specs=VMEM,
        compiler_params=params(),
        cost_estimate=cost(2 * SLOTS * MEMBERS * QUARTER, 2_000_000),
        name="dots",
    )(arrived, resident, factor)

    partial = partial.reshape(DOCS, 2, 4, SHARE).transpose(0, 2, 1, 3).reshape(4 * DOCS, 2, SHARE)
    returned = lax.all_to_all(partial, ALL, split_axis=0, concat_axis=0, tiled=True)
    returned = returned.reshape(4 * SLOTS, SHARE)
    scores, best = pl.pallas_call(
        home_kernel,
        out_shape=(
            jax.ShapeDtypeStruct((DOCS, SHARE), F32),
            jax.ShapeDtypeStruct((8, 128), F32),
        ),
        in_specs=[VMEM] * 4,
        out_specs=(VMEM, VMEM),
        compiler_params=params(),
        cost_estimate=cost(2 * SLOTS * DOCS * SHARE, 400_000),
        name="home",
    )(returned, pick, scale, live)
    return scores, lax.pmax(best[0], "tensor")


def gain_of(norm_gain, x):
    return lax.dynamic_slice(norm_gain, (x * QUARTER,), (QUARTER,)).reshape(1, QUARTER)


def solution(mesh):
    split = Mesh(mesh.devices.reshape(8, 8, 2, 4), ALL)
    in_specs = (
        P(DP, "tensor"),
        P(ALL, None),
        P("tensor", DP),
        P(),
        P(DP, None, "tensor"),
        P(ALL, None),
        P(DP, None),
        P(),
        P(),
    )
    out_specs = (P(DP, "tensor"), P(DP))
    return jax.shard_map(body, mesh=split, in_specs=in_specs, out_specs=out_specs, check_vma=False)
```

```python
import jax
import jax.numpy as jnp
from jax import lax
from jax.experimental import pallas as pl
from jax.experimental.pallas import tpu as pltpu
from jax.sharding import Mesh, PartitionSpec as P

DP = ("z", "y", "core")
ALL = ("z", "y", "core", "tensor")
BF = jnp.bfloat16
F32 = jnp.float32
NT = (((1,), (1,)), ((), ()))
SMEM = pl.BlockSpec(memory_space=pltpu.SMEM)
VMEM = pl.BlockSpec(memory_space=pltpu.VMEM)
TOK, QUARTER, HALF = 512, 896, 448
DOCS, SLOTS, MEMBERS, SHARE = 128, 256, 512, 128


def params(mib=20):
    return pltpu.CompilerParams(vmem_limit_bytes=mib * 1024 * 1024)


def cost(flops, nbytes):
    return pl.CostEstimate(flops=flops, bytes_accessed=nbytes, transcendentals=0)


def device(z, y, core, x):
    return ((z * 8 + y) * 2 + core) * 4 + x


def placed(core, ring, line):
    return (ring, line) if core == 0 else (line, ring)


def grid():
    return [(z, y, c, x) for z in range(8) for y in range(8) for c in range(2) for x in range(4)]


def spread(flip):
    pairs = []
    for z, y, core, x in grid():
        to = core ^ flip
        to_z, to_y = placed(to, 2 * x + z % 2, y)
        pairs.append((device(z, y, core, x), device(to_z, to_y, to, z // 2)))
    return pairs


def groups(along):
    found = []
    for core in range(2):
        for x in range(4):
            for other in range(8):
                over_z = (along == "ring") == (core == 0)
                found.append(
                    [device(i, other, core, x) if over_z else device(other, i, core, x) for i in range(8)]
                )
    return found


def pair(value, turn):
    pairs = []
    for z, y, core, x in grid():
        pairs.append((device(z, y, core, x), device(z, y, core, x ^ (1 if core == turn else 3))))
    return lax.ppermute(value, ALL, pairs)


def core_swap(value):
    return lax.ppermute(value, ALL, [(at, at ^ 4) for at in range(512)])


def pack_kernel(place, context, residual, small, near, rest, side):
    for out, row, target in ((near, 0, 1), (near, 128, 3), (side, 512, 2)):
        start = pl.multiple_of(place[target] * QUARTER, 128)
        out[row : row + 128, :] = residual[:, pl.ds(start, QUARTER)]
    near[256:272, :] = small[...]
    near[272:400, :] = context[0:128, :]
    rest[...] = context[128:TOK, :]
    side[0:TOK, :] = context[...]
    side[640:656, :] = small[...]


def project_kernel(
    place, context, near, near_rest, side, far, far_rest, weight, res, hidden, squares,
    ctx, tails, blocks, sems,
):
    def fetch(source, target, at):
        return pltpu.make_async_copy(source, target, sems.at[at])

    pieces = (
        ((context, 0, 0, TOK),),
        ((near, 272, 0, 128), (near_rest, 0, 128, 384)),
        ((side, 0, 0, TOK),),
        ((far, 272, 0, 128), (far_rest, 0, 128, 384)),
    )
    copies, used = [], 0
    for index, parts in enumerate(pieces):
        start = pl.multiple_of(place[index] * QUARTER, QUARTER)
        group = [fetch(weight.at[pl.ds(start, QUARTER), :], blocks.at[index], used)]
        used += 1
        for piece, row, to, count in parts:
            group.append(
                fetch(piece.at[pl.ds(row, count), :], ctx.at[index, pl.ds(to, count), :], used)
            )
            used += 1
        copies.append(group)
    ends = [
        fetch(piece.at[pl.ds(row, 128), :], tails.at[index], used + index)
        for index, (piece, row) in enumerate(((res, 0), (near, 0), (side, 512), (far, 128)))
    ]
    for pair_of in copies:
        for copy in pair_of:
            copy.start()
    for copy in ends:
        copy.start()
    for index in range(4):
        for copy in copies[index]:
            copy.wait()
        product = lax.dot_general(ctx[index], blocks[index], NT, preferred_element_type=F32)
        if index == 0:
            hidden[...] = product
        else:
            hidden[...] += product
    for copy in ends:
        copy.wait()
    squares[...] = jnp.zeros_like(squares)
    for index in range(4):
        at = place[index]
        rows = pl.ds(pl.multiple_of(at * 128, 128), 128)
        value = hidden[rows, :] + tails[index].astype(F32)
        hidden[rows, :] = value
        sq = value * value
        part = sq[:, 0:128]
        for tile in range(1, 7):
            part = part + sq[:, tile * 128 : tile * 128 + 128]
        squares[pl.ds(at, 1), :] = jnp.sum(part.T, axis=0, keepdims=True)


def pool_kernel(hidden, gain, pool, inverse, total, slots, squares):
    scale = lax.rsqrt(total[...] / 3584.0 + 1e-06)
    summed = None
    for pack in range(4):
        rows = pl.ds(pack * 128, 128)
        column = jnp.broadcast_to(scale[pack : pack + 1, :], (128, 128)).T
        column = jnp.concatenate([column] * 7, axis=1)
        normed = (hidden[rows, :] * column * gain[...]).astype(BF)
        term = jnp.dot(pool[:, pack * 128 : pack * 128 + 128], normed, preferred_element_type=F32)
        summed = term if summed is None else summed + term
    pooled = summed * jnp.concatenate([inverse[...]] * 7, axis=1)
    slots[...] = pooled.astype(BF)
    sq = pooled * pooled
    part = sq[:, 0:128]
    for tile in range(1, 7):
        part = part + sq[:, tile * 128 : tile * 128 + 128]
    squares[...] = jnp.zeros_like(squares)
    for block in range(2):
        squares[pl.ds(block, 1), :] = jnp.sum(
            part[block * 128 : block * 128 + 128, :].T, axis=0, keepdims=True
        )


def dots_kernel(arrived, members, factor, out):
    for part in range(4):
        rows = pl.ds(part * SHARE, SHARE)
        dots = lax.dot_general(arrived[...], members[rows, :], NT, preferred_element_type=F32)
        out[:, part * SHARE : part * SHARE + SHARE] = (dots * factor[pl.ds(part, 1), :]).astype(BF)


def home_kernel(returned, pick, scale, live, scores, best):
    rows = jnp.dot(pick[...], returned[...], preferred_element_type=F32) * scale[...]
    scores[...] = rows
    masked = jnp.where(live[...] > 0.0, rows, -1000000000.0)
    best[...] = jnp.broadcast_to(jnp.max(masked.T, axis=0, keepdims=True), (8, 128))


def body(
    context,
    residual,
    out_weight,
    norm_gain,
    members,
    doc_lengths,
    doc_cluster,
    owner_map,
    member_counts,
):
    z, y = lax.axis_index("z"), lax.axis_index("y")
    core, x = lax.axis_index("core"), lax.axis_index("tensor")

    first = core == 0
    near_x = jnp.where(first, x ^ 1, x ^ 3)
    side_x = jnp.where(first, x ^ 3, x ^ 1)
    far_x = x ^ 2
    place = jnp.stack([x, near_x, side_x, far_x]).astype(jnp.int32)

    weight = out_weight.T
    keep = lax.ppermute(weight, ALL, spread(0))
    cross = lax.ppermute(weight, ALL, spread(1))
    block = jnp.concatenate(
        [jnp.where(first, keep, cross), jnp.where(first, cross, keep)], axis=0
    )

    resident = members[0]
    resident_f = resident.astype(F32)
    partial_sq = jnp.sum(resident_f * resident_f, axis=-1).astype(BF)
    small = jnp.concatenate(
        [partial_sq.reshape(4, 128), jnp.pad(doc_lengths.astype(BF), ((0, 0), (0, 96)))], axis=0
    )
    small = jnp.pad(small, ((0, 11), (0, QUARTER - 128)))
    to_near, to_rest, to_side = pl.pallas_call(
        pack_kernel,
        out_shape=(
            jax.ShapeDtypeStruct((400, QUARTER), BF),
            jax.ShapeDtypeStruct((384, QUARTER), BF),
            jax.ShapeDtypeStruct((656, QUARTER), BF),
        ),
        in_specs=[SMEM] + [VMEM] * 3,
        out_specs=(pl.BlockSpec(),) * 3,
        compiler_params=params(),
        cost_estimate=cost(0, 6_000_000),
        name="pack",
    )(place, context, residual, small)

    near = pair(to_near, 0)
    plane = lax.all_to_all(
        jnp.broadcast_to(block[None], (8, 56, QUARTER)), ALL, 0, 0,
        axis_index_groups=groups("line"), tiled=True,
    ).reshape(HALF, QUARTER)
    plane, near, _, _ = lax.optimization_barrier((plane, near, to_rest, to_side))
    plane = lax.all_gather(plane, ALL, axis=0, axis_index_groups=groups("ring"), tiled=True)
    near_rest, far = pair(to_rest, 0), pair(near, 1)
    near_rest, late_side = lax.optimization_barrier((near_rest, to_side))
    far_rest, side = pair(near_rest, 1), pair(late_side, 1)

    tails = [(x, small), (near_x, near[256:272]), (side_x, side[-16:]), (far_x, far[256:272])]
    member_sq = sum((tail[:4, :128].astype(F32) for _, tail in tails[1:]), small[:4, :128].astype(F32))
    lens = jnp.zeros((4, 32), F32)
    for at, tail in tails:
        lens = lax.dynamic_update_slice(lens, tail[4:5, :32].astype(F32), (at, 0))

    cluster_ids = jnp.arange(owner_map.shape[0], dtype=jnp.int32)
    matches = doc_cluster[:, 0][:, None] == cluster_ids[None, :]
    doc_owner = jnp.sum(jnp.where(matches, owner_map[None, :], 0), axis=1)
    doc_members = jnp.sum(jnp.where(matches, member_counts[None, :], 0), axis=1)
    doc_order = jnp.arange(DOCS, dtype=jnp.int32)
    same_owner = (doc_owner[:, None] == doc_owner[None, :]) & (
        doc_order[:, None] > doc_order[None, :]
    )
    doc_slot = doc_owner * 2 + jnp.sum(same_owner.astype(jnp.int32), axis=1)
    slot_ids = jnp.arange(SLOTS, dtype=jnp.int32)
    select = slot_ids[:, None] == doc_slot[None, :]
    wide_ids = jnp.arange(4 * SLOTS, dtype=jnp.int32)
    wide_ids = lax.div(wide_ids, 8) * 2 + lax.rem(wide_ids, 2)
    pick = (doc_slot[:, None] == wide_ids[None, :]).astype(BF)
    lens_int = lens.astype(jnp.int32)
    ends = jnp.cumsum(lens_int, axis=1)
    offsets = 128 * jnp.arange(4, dtype=jnp.int32)[:, None]
    doc_begin = (ends - lens_int + offsets).reshape(DOCS)
    doc_end = (ends + offsets).reshape(DOCS)
    tokens = jnp.arange(TOK, dtype=jnp.int32)
    inside = (tokens[None, :] >= doc_begin[:, None]) & (tokens[None, :] < doc_end[:, None])
    pool = jnp.dot(select.astype(BF), inside.astype(BF), preferred_element_type=F32).astype(BF)
    slot_len = jnp.sum(jnp.where(select, lens.reshape(DOCS)[None, :], 0.0), axis=1)
    inverse = jnp.broadcast_to((1.0 / jnp.maximum(slot_len, 1.0))[:, None], (SLOTS, 128))
    columns = x * SHARE + jnp.arange(SHARE, dtype=jnp.int32)
    live = (columns[None, :] < doc_members[:, None]).astype(F32)

    own_dp = (z * 8 + y) * 2 + core
    own_count = jnp.sum(jnp.where(owner_map == own_dp, member_counts, 0))
    member_ids = jnp.arange(MEMBERS, dtype=jnp.int32).reshape(4, 128)
    factor = jnp.where(member_ids < own_count, lax.rsqrt(member_sq / 3584.0 + 1e-06), 0.0)

    res = lax.dynamic_slice(residual, (0, x * QUARTER), (128, QUARTER))
    hidden, squares = pl.pallas_call(
        project_kernel,
        out_shape=(
            jax.ShapeDtypeStruct((TOK, QUARTER), F32),
            jax.ShapeDtypeStruct((8, 128), F32),
        ),
        in_specs=[SMEM] + [pl.BlockSpec(memory_space=pl.ANY)] * 8,
        out_specs=(VMEM, VMEM),
        scratch_shapes=[
            pltpu.VMEM((4, TOK, QUARTER), BF),
            pltpu.VMEM((4, 128, QUARTER), BF),
            pltpu.VMEM((4, QUARTER, QUARTER), BF),
            pltpu.SemaphoreType.DMA((14,)),
        ],
        compiler_params=params(50),
        cost_estimate=cost(2 * TOK * QUARTER * 3584, 13_000_000),
        name="project",
    )(place, context, near, near_rest, side, far, far_rest, plane, res)

    slots, doc_sq = pl.pallas_call(
        pool_kernel,
        out_shape=(
            jax.ShapeDtypeStruct((SLOTS, QUARTER), BF),
            jax.ShapeDtypeStruct((8, 128), F32),
        ),
        in_specs=[VMEM] * 5,
        out_specs=(VMEM, VMEM),
        compiler_params=params(),
        cost_estimate=cost(2 * SLOTS * TOK * QUARTER, 3_000_000),
        name="pool",
    )(hidden, gain_of(norm_gain, x), pool, inverse, lax.psum(squares, "tensor"))

    arrived = lax.all_to_all(
        slots.reshape(DOCS, 2, QUARTER), DP, split_axis=0, concat_axis=0, tiled=True
    ).reshape(SLOTS, QUARTER)

    slot_sq = lax.psum(doc_sq, "tensor")[:2].reshape(SLOTS)
    doc_total = jnp.sum(jnp.where(select, slot_sq[:, None], 0.0), axis=0)
    scale = jnp.broadcast_to(lax.rsqrt(doc_total + 1e-06)[:, None], (DOCS, SHARE))

    partial = pl.pallas_call(
        dots_kernel,
        out_shape=jax.ShapeDtypeStruct((SLOTS, MEMBERS), BF),
        in_specs=[VMEM] * 3,
        out_specs=VMEM,
        compiler_params=params(),
        cost_estimate=cost(2 * SLOTS * MEMBERS * QUARTER, 2_000_000),
        name="dots",
    )(arrived, resident, factor)

    partial = partial.reshape(DOCS, 2, 4, SHARE).transpose(0, 2, 1, 3).reshape(4 * DOCS, 2, SHARE)
    returned = lax.all_to_all(partial, ALL, split_axis=0, concat_axis=0, tiled=True)
    returned = returned.reshape(4 * SLOTS, SHARE)
    scores, best = pl.pallas_call(
        home_kernel,
        out_shape=(
            jax.ShapeDtypeStruct((DOCS, SHARE), F32),
            jax.ShapeDtypeStruct((8, 128), F32),
        ),
        in_specs=[VMEM] * 4,
        out_specs=(VMEM, VMEM),
        compiler_params=params(),
        cost_estimate=cost(2 * SLOTS * DOCS * SHARE, 400_000),
        name="home",
    )(returned, pick, scale, live)
    return scores, lax.pmax(best[0], "tensor")


def gain_of(norm_gain, x):
    return lax.dynamic_slice(norm_gain, (x * QUARTER,), (QUARTER,)).reshape(1, QUARTER)


def solution(mesh):
    split = Mesh(mesh.devices.reshape(8, 8, 2, 4), ALL)
    in_specs = (
        P(DP, "tensor"),
        P(ALL, None),
        P("tensor", DP),
        P(),
        P(DP, None, "tensor"),
        P(ALL, None),
        P(DP, None),
        P(),
        P(),
    )
    out_specs = (P(DP, "tensor"), P(DP))
    return jax.shard_map(body, mesh=split, in_specs=in_specs, out_specs=out_specs, check_vma=False)
```
